128 devices in a mesh: dp: 16 (over y, x), tensor: 8 (over z, core).
Axes of the slice: x: 4, y: 4, z: 4, core: 2. Of those that a mesh axis runs over, the one named last changes fastest.
Arguments:
- inputs: bfloat16 [16384, 2048], P('dp'), may hold values from -6 to 6
- norm_gain: bfloat16 [2048], replicated, may hold values from 0.5 to 1.5
- norm_bias: bfloat16 [2048], replicated, may hold values from -3 to 3
- attn_weight: bfloat16 [3, 2048, 2048], P(None, None, 'tensor'), may hold values from -0.1875 to 0.1875
- attn_bias: bfloat16 [3, 2048], P(None, 'tensor'), may hold values from -3 to 3
- dense_weight: bfloat16 [2048, 2048], P('tensor'), may hold values from -1.5 to 1.5
- dense_bias: bfloat16 [2048], replicated, may hold values from -3 to 3
- expand_weight: bfloat16 [2048, 8192], P(None, 'tensor'), may hold values from -0.125 to 0.125
- expand_bias: bfloat16 [8192], P('tensor'), may hold values from -3 to 3
- shrink_weight: bfloat16 [8192, 2048], P('tensor'), may hold values from -0.0625 to 0.0625
- shrink_bias: bfloat16 [2048], replicated, may hold values from -3 to 3
- cotangent: bfloat16 [16384, 2048], P('dp'), may hold values from -6 to 6
Outputs:
- output: bfloat16 [16384, 2048], P('dp')
- input_grad: float32 [16384, 2048], P('dp')
- gain_grad: float32 [2048], P('dp')
- shift_grad: float32 [2048], P('dp')
- attn_weight_grad: float32 [3, 2048, 2048], P(None, 'dp', 'tensor')
- attn_bias_grad: float32 [3, 2048], P(None, ('tensor', 'dp'))
- dense_weight_grad: float32 [2048, 2048], P('tensor', 'dp')
- dense_bias_grad: float32 [2048], P('dp')
- expand_weight_grad: float32 [2048, 8192], P('dp', 'tensor')
- expand_bias_grad: float32 [8192], P(('tensor', 'dp'))
- shrink_weight_grad: float32 [8192, 2048], P('tensor', 'dp')
- shrink_bias_grad: float32 [2048], P('dp')
The draws below stay inside these ranges and needn't reach their ends.
All inputs are finite; a program needn't handle non-finite values.
Results may differ from the reference program's by a relative error of at most 0.005.
The reference program's roundings to bfloat16 on the way count: a program that leaves them out, or rounds other values in their place, can miss the bound.
Values sent between devices are 32-bit elements; how exact they have to be, the bound alone decides.
A program may use at most 192 MiB of HBM per device.

```python
import jax
import jax.numpy as jnp
from jax import lax

D = 2048
H = 32
HD = 64
ROT = 32
FF = 8192
LENGTH = 1024
TOKENS = 16384


def spiked(values, stream_key, source, target, blocks, factor):
    def block_of(dim):
        return (jnp.arange(values.shape[dim]) // (values.shape[dim] // blocks)).reshape((-1,) + (1,) * (values.ndim - 1 - dim))

    first = jax.random.permutation(stream_key, blocks)[block_of(target)]
    other_side = (block_of(target) + blocks // 2) % blocks
    return jnp.where((block_of(source) == first) | (block_of(source) == other_side), factor * values, values)


def block_levels(stream_key, shape, pieces, low, largest):
    loudness = 1.0
    for position, shards_of in pieces:
        draws = jax.random.uniform(jax.random.fold_in(jax.random.fold_in(stream_key, 6), position), (shards_of,), jnp.float32, low / len(pieces), largest / len(pieces))
        loudness = loudness * jnp.repeat(jnp.exp(draws), shape[position] // shards_of).reshape((-1,) + (1,) * (len(shape) - 1 - position))
    return loudness


def bell_draw(own_key, dims, deviation, most, shards=(), held_as=jnp.bfloat16):
    values = jax.random.normal(own_key, dims, jnp.float32) * deviation
    if len(shards) > 0:
        values = block_levels(own_key, dims, shards, -0.22, 0.18) * values
    return jnp.clip(values, min=-most, max=most).astype(held_as)


def bell_draw_with(rng, shape, deviation, most, split, heavy, kind=jnp.bfloat16):
    drawn = deviation * jax.random.normal(rng, shape, jnp.float32)
    if split:
        drawn = drawn * block_levels(rng, shape, split, -0.22, 0.18)
    return jnp.clip(spiked(drawn, jax.random.fold_in(rng, 3), *heavy), -most, most).astype(kind)


def setup_inputs(seed: int = 0) -> dict:
    key_list = jax.random.split(jax.random.key(seed), 13)
    return {
        "inputs": bell_draw(key_list[0], (TOKENS, D), 1.0, 6.0, ((0, 16),)),
        "norm_gain": jnp.clip(1.0 + 0.1 * jax.random.normal(key_list[1], (D,), jnp.float32), 0.5, 1.5).astype(jnp.bfloat16),
        "norm_bias": bell_draw(key_list[2], (D,), 0.3, 3.0),
        "attn_weight": bell_draw(key_list[3], (3, D, D), (D // 2) ** -0.5, 0.1875, ((2, 8),)),
        "attn_bias": bell_draw(key_list[4], (3, D), 0.3, 3.0, ((1, 8),)),
        "dense_weight": bell_draw(key_list[5], (D, D), (max(1, D // 128)) ** -0.5, 1.5, ((0, 8),)),
        "dense_bias": bell_draw(key_list[6], (D,), 0.5, 3.0),
        "expand_weight": bell_draw(key_list[7], (D, FF), D ** -0.5, 0.125, ((1, 8),)),
        "expand_bias": bell_draw(key_list[8], (FF,), 0.5, 3.0, ((0, 8),)),
        "shrink_weight": bell_draw(key_list[9], (FF, D), FF ** -0.5, 0.0625, ((0, 8),)),
        "shrink_bias": bell_draw(key_list[10], (D,), 0.5, 3.0),
        "cotangent": bell_draw_with(key_list[11], (TOKENS, D), 1.0, 6.0, ((0, 16),), (0, 1, 16, 2.0)),
    }


precise = lax.Precision.HIGHEST
rotary_base = 10000.0
norm_eps = 1e-05

@jax.custom_vjp
def low(v):
    return lax.optimization_barrier(v.astype(jnp.bfloat16)).astype(jnp.float32)

@jax.custom_vjp
def low_back(v):
    return v

def low_keep(v):
    return (low(v), None)

def low_pass(kept, grad):
    return (grad,)

def back_keep(v):
    return (v, None)

def back_low(kept, grad):
    return (low(grad),)
low.defvjp(low_keep, low_pass)
low_back.defvjp(back_keep, back_low)

def layer_norm(values, gain, shift):
    center = lax.optimization_barrier(jnp.mean(values, axis=-1, keepdims=True))
    centred = values - center
    spread = lax.optimization_barrier(jnp.mean(centred * centred, axis=-1, keepdims=True))
    return centred * lax.rsqrt(spread + norm_eps) * gain + shift

def gelu_tanh(values):
    return 0.5 * values * (1.0 + jnp.tanh(0.7978845608 * (values + 0.044715 * values * values * values)))

def rotary_tables(length, rot_dims):
    halfway = rot_dims // 2
    powers = jnp.arange(halfway).astype(jnp.float32) * (2.0 / rot_dims)
    freqs = jnp.exp(-powers * jnp.log(jnp.float32(rotary_base)).astype(powers.dtype))
    angles = jnp.arange(length).astype(jnp.float32)[:, None] * freqs[None, :]
    angles = jnp.concatenate([angles, angles], axis=1)
    return (jnp.cos(angles), jnp.sin(angles))

def rotate_heads(heads, cosine, sine, rot_dims):
    halfway = rot_dims // 2
    turned_part = heads[..., :rot_dims]
    swapped = jnp.concatenate([-turned_part[..., halfway:], turned_part[..., :halfway]], axis=-1)
    result = turned_part * cosine[:, None, :] + swapped * sine[:, None, :]
    return jnp.concatenate([result, heads[..., rot_dims:]], axis=-1)

def forward(states, params):
    gain, shift, attn_w, attn_b, dense_w, dense_b, expand_w, expand_b, shrink_w, shrink_b = params
    normed = low(layer_norm(states, gain, shift))
    proj = jnp.einsum('td,kde->kte', normed, attn_w, precision=precise) + attn_b[:, None, :]
    proj = low_back(proj).reshape(3, LENGTH, H, HD)
    cosine, sine = rotary_tables(LENGTH, ROT)
    query = low(rotate_heads(proj[0], cosine, sine, ROT))
    keys = low(rotate_heads(proj[1], cosine, sine, ROT))
    values = low(proj[2])
    scores = jnp.einsum('qhd,khd->hqk', query, keys, precision=precise) * HD ** (-0.5)
    scores = low_back(scores)
    allowed = jnp.arange(LENGTH)[None, :] <= jnp.arange(LENGTH)[:, None]
    scores = jnp.where(allowed[None], scores, -1e+30)
    row_top = lax.optimization_barrier(jnp.max(scores, axis=-1, keepdims=True))
    expo = jnp.exp(scores - row_top)
    chances = low(expo / lax.optimization_barrier(jnp.sum(expo, axis=-1, keepdims=True)))
    attended = jnp.einsum('hqk,khd->qhd', chances, values, precision=precise).reshape(LENGTH, D)
    attended = low(low_back(attended))
    attn_part = jnp.dot(attended, dense_w, precision=precise)
    hidden = low_back(jnp.dot(normed, expand_w, precision=precise) + expand_b)
    act = low(gelu_tanh(hidden))
    mlp_part = jnp.dot(act, shrink_w, precision=precise)
    return states + attn_part + mlp_part + dense_b + shrink_b

def reference(inputs, norm_gain, norm_bias, attn_weight, attn_bias, dense_weight, dense_bias, expand_weight, expand_bias, shrink_weight, shrink_bias, cotangent):
    params = tuple((p.astype(jnp.float32) for p in (norm_gain, norm_bias, attn_weight, attn_bias, dense_weight, dense_bias, expand_weight, expand_bias, shrink_weight, shrink_bias)))
    states_all = inputs.astype(jnp.float32).reshape(-1, LENGTH, D)
    grads_all = cotangent.astype(jnp.float32).reshape(-1, LENGTH, D)

    def one_sequence(totals, pair):
        states, grads = pair
        result, back = jax.vjp(forward, states, params)
        grad_states, grad_params = back(grads)
        totals = jax.tree.map(jnp.add, totals, grad_params)
        return (totals, (result, grad_states))
    zeros = jax.tree.map(jnp.zeros_like, params)
    totals, (results, grad_inputs) = lax.scan(one_sequence, zeros, (states_all, grads_all))
    return (results.reshape(TOKENS, D).astype(jnp.bfloat16), grad_inputs.reshape(TOKENS, D), totals[0], totals[1], totals[2], totals[3], totals[4], totals[5], totals[6], totals[7], totals[8], totals[9])
```

```python
import functools

import jax
import jax.numpy as jnp
from jax import lax
from jax.experimental import pallas as pl
from jax.experimental.pallas import tpu as pltpu
from jax.sharding import PartitionSpec as P

HD = 64
ROT = 32
LENGTH = 1024
D = 2048
F32 = jnp.float32
BF16 = jnp.bfloat16
MESH = pl.DeviceIdType.MESH

rotary_base = 10000.0
norm_eps = 1e-05

UNITS = 16
UROWS = 128
BATCHES = 16
BROWS = 192
KX = 5
KZ = 6
TICKS = 21


def layer_kernel(
    x_ref, g_ref, n_ref, act_ref, att_ref, gh_ref, gp_ref, sw_ref, dw_ref, ew_ref, aw_ref,
    vec_ref,
    go_ref, gi_ref, f_ref, gs_ref,
    stream, turned, part, core_in, mine, zp, zd, zb, done,
    xp, xd, xb, mid, yp, yd, yb,
    xsend, xrecv, ysend, yrecv, csend, crecv, zsend, zrecv, gsend, grecv, ssend, srecv, lsem,
):
    dp = lax.axis_index("dp")
    tn = lax.axis_index("tensor")
    x, y, c, z = dp % 4, dp // 4, tn % 2, tn // 2

    def side(axis, sg):
        if axis == 0:
            return (y * 4 + (x + sg + 4) % 4, tn)
        if axis == 1:
            return (((y + sg + 4) % 4) * 4 + x, tn)
        if axis == 2:
            return (dp, ((z + sg + 4) % 4) * 2 + c)
        return (dp, z * 2 + 1 - c)

    SIDES = [(0, 1), (0, -1), (1, 1), (1, -1), (2, 1), (2, -1), (3, 0)]
    barrier = pltpu.get_barrier_semaphore()
    for axis, sg in SIDES:
        pl.semaphore_signal(barrier, inc=1, device_id=side(axis, sg), device_id_type=MESH)

    gs_ref[...] = jnp.zeros_like(gs_ref)

    def remote(src, dst, ssem, rsem, to):
        return pltpu.make_async_remote_copy(
            src_ref=src, dst_ref=dst, send_sem=ssem, recv_sem=rsem, device_id=to, device_id_type=MESH
        )

    SG = (1, -1)
    HALVES = (0, 1)

    def rows_of(b, h, hh):
        return pl.ds(pl.multiple_of((b % 4) * BROWS + h * 96 + hh * 48, 8), 48)

    def own_rows(b, h, piece, hh):
        return (
            stream.at[:, piece, rows_of(b, h, hh)]
            if h == 0
            else stream.at[piece, :, rows_of(b, h, hh)]
        )

    def first(kind, h, d, b):
        a = (x, y)[h]
        sg = SG[d]
        slot = b % KX
        sems = (xsend.at[kind, h, d, slot], xrecv.at[kind, h, d, slot], side(h, sg))
        if kind == 0:
            return remote(own_rows(b, h, (a + 2) % 4, d), xp.at[h, d, slot], *sems)
        if kind == 1:
            return remote(own_rows(b, h, (a + sg + 4) % 4, 1 - d), xd.at[h, d, slot], *sems)
        return remote(xp.at[h, d, slot], xb.at[h, d, slot], *sems)

    def second(kind, h, d, b):
        a = (y, x)[h]
        sg = SG[d]
        slot = b % KX
        sems = (ysend.at[kind, h, d, slot], yrecv.at[kind, h, d, slot], side(1 - h, sg))
        if kind == 0:
            return remote(mid.at[h, slot, (a + 2) % 4, pl.ds(d * 48, 48)], yp.at[h, d, slot], *sems)
        if kind == 1:
            return remote(
                mid.at[h, slot, (a + sg + 4) % 4, pl.ds((1 - d) * 48, 48)], yd.at[h, d, slot], *sems
            )
        return remote(yp.at[h, d, slot], yb.at[h, d, slot], *sems)

    def each(make, kinds, b):
        for kind in kinds:
            for h in HALVES:
                for d in (0, 1):
                    yield make(kind, h, d, b)

    def x0(b):
        for copy in each(first, (0, 1), b):
            copy.start()

    def x1(b):
        slot = b % KX
        for h in HALVES:
            for d in (0, 1):
                a = (x, y)[h]
                first(0, h, d, b).wait_recv()
                xp[h, d, slot] = xp[h, d, slot] + own_rows(b, h, (a + SG[d] + 4) % 4, d)[...]
                first(2, h, d, b).start()

    def x2(b):
        slot = b % KX
        for h in HALVES:
            a = (x, y)[h]
            for d in (0, 1):
                first(1, h, d, b).wait_recv()
                first(2, h, d, b).wait_recv()
            for hh in (0, 1):
                mid[h, slot, :, pl.ds(hh * 48, 48)] = (
                    own_rows(b, h, a, hh)[...] + xb[h, hh, slot] + xd[h, 1 - hh, slot]
                )
            for kind in (0, 1):
                for d in (0, 1):
                    second(kind, h, d, b).start()
        for copy in each(first, (0, 1, 2), b):
            copy.wait_send()

    def x3(b):
        slot = b % KX
        for h in HALVES:
            a = (y, x)[h]
            for d in (0, 1):
                second(0, h, d, b).wait_recv()
                yp[h, d, slot] = (
                    yp[h, d, slot] + mid[h, slot, (a + SG[d] + 4) % 4, pl.ds(d * 48, 48)]
                )
                second(2, h, d, b).start()

    def x4(b):
        slot = b % KX
        for h in HALVES:
            a = (y, x)[h]
            for d in (0, 1):
                second(1, h, d, b).wait_recv()
                second(2, h, d, b).wait_recv()
            for hh in (0, 1):
                at = pl.ds(pl.multiple_of(b * BROWS + h * 96 + hh * 48, 8), 48)
                f_ref[at] = mid[h, slot, a, pl.ds(hh * 48, 48)] + yb[h, hh, slot] + yd[h, 1 - hh, slot]
        for copy in each(second, (0, 1, 2), b):
            copy.wait_send()

    def zrows(u, piece, hh):
        return mine.at[u % 3, pl.ds(pl.multiple_of(piece * 16 + hh * 8, 8), 8)]

    def along(kind, d, u):
        sg = SG[d]
        slot = u % KZ
        sems = (zsend.at[kind, d, slot], zrecv.at[kind, d, slot], side(2, sg))
        if kind == 0:
            return remote(zrows(u, (z + 2) % 4, d), zp.at[d, slot], *sems)
        if kind == 1:
            return remote(zrows(u, (z + sg + 4) % 4, 1 - d), zd.at[d, slot], *sems)
        return remote(zp.at[d, slot], zb.at[d, slot], *sems)

    def cross(u):
        return remote(
            part.at[u % 2, pl.ds(pl.multiple_of((1 - c) * 64, 64), 64)],
            core_in.at[u % 2],
            csend.at[u % 2],
            crecv.at[u % 2],
            side(3, 0),
        )

    def grow(u, cc, piece, off, size):
        return pl.ds(pl.multiple_of((u % 8) * UROWS + cc * 64 + piece * 16 + off, 8), size)

    def gather1(ref, d, u):
        slot = u % KZ
        return remote(
            done.at[u % 2], ref.at[grow(u, c, z, 0, 16)], gsend.at[0, d, slot], grecv.at[0, d, slot],
            side(2, SG[d]),
        )

    def gather2(ref, d, u):
        slot = u % KZ
        at = grow(u, c, (z - SG[d] + 4) % 4, d * 8, 8)
        return remote(
            ref.at[at], ref.at[at], gsend.at[1, d, slot], grecv.at[1, d, slot], side(2, SG[d])
        )

    def twin(ref, k, u):
        slot = u % KZ
        at = grow(u, c, (z + (0, -1, 1, 2)[k] + 4) % 4, 0, 16)
        src = done.at[u % 2] if k == 0 else ref.at[at]
        return remote(src, ref.at[at], ssend.at[k, slot], srecv.at[k, slot], side(3, 0))

    def keep(ref, u):
        return pltpu.make_async_copy(done.at[u % 2], ref.at[grow(u, c, z, 0, 16)], lsem.at[u % 2])

    def on_ref(u, body):
        @pl.when(u < 8)
        def _():
            body(go_ref)

        @pl.when(u >= 8)
        def _():
            body(gi_ref)

    def z0(u):
        rows = pl.ds(pl.multiple_of((u % 8) * UROWS, UROWS), UROWS)

        @pl.when(u < 8)
        def _():
            @pl.loop(0, 4)
            def _(j):
                cols = pl.ds(pl.multiple_of(j * 512, 512), 512)
                part[u % 2, :, cols] = jnp.dot(
                    act_ref[rows, :], sw_ref[:, cols], preferred_element_type=F32
                ) + jnp.dot(att_ref[rows, :], dw_ref[:, cols], preferred_element_type=F32)

        @pl.when(u >= 8)
        def _():
            nt = (((1,), (1,)), ((), ()))

            @pl.loop(0, 4)
            def _(j):
                cols = pl.ds(pl.multiple_of(j * 512, 512), 512)
                total = lax.dot_general(
                    gh_ref[rows, :], ew_ref[cols, :], nt, preferred_element_type=F32
                )
                for k in range(3):
                    total += lax.dot_general(
                        gp_ref[k, rows, :], aw_ref[k, cols, :], nt, preferred_element_type=F32
                    )
                part[u % 2, :, cols] = total

        cross(u).start()

    def z1(u):
        cross(u).wait_recv()
        mine[u % 3] = part[u % 2, pl.ds(pl.multiple_of(c * 64, 64), 64)] + core_in[u % 2]
        for kind in (0, 1):
            for d in (0, 1):
                along(kind, d, u).start()

    def z2(u):
        slot = u % KZ
        for d in (0, 1):
            along(0, d, u).wait_recv()
            zp[d, slot] = zp[d, slot] + zrows(u, (z + SG[d] + 4) % 4, d)[...]
            along(2, d, u).start()
        cross(u).wait_send()

    def z3(u):
        slot = u % KZ
        for d in (0, 1):
            along(1, d, u).wait_recv()
            along(2, d, u).wait_recv()
        whole = jnp.concatenate(
            [zrows(u, z, hh)[...] + zb[hh, slot] + zd[1 - hh, slot] for hh in (0, 1)], axis=0
        )
        rows = pl.ds(pl.multiple_of((u % 8) * UROWS + c * 64 + z * 16, 16), 16)
        states = x_ref[rows, :].astype(F32)

        @pl.when(u < 8)
        def _():
            done[u % 2] = states + whole + vec_ref[1:2, :]

        @pl.when(u >= 8)
        def _():
            center = jnp.mean(states, axis=-1, keepdims=True)
            centred = states - center
            spread = jnp.mean(centred * centred, axis=-1, keepdims=True)
            r = lax.rsqrt(spread + norm_eps)
            zz = centred * r
            e = whole * vec_ref[0:1, :]
            done[u % 2] = g_ref[rows, :].astype(F32) + r * (
                e
                - jnp.mean(e, axis=-1, keepdims=True)
                - zz * jnp.mean(e * zz, axis=-1, keepdims=True)
            )
            gs_ref[0:1, :] += jnp.sum(whole * zz, axis=0, keepdims=True)
            gs_ref[1:2, :] += jnp.sum(whole, axis=0, keepdims=True)

        def send(ref):
            keep(ref, u).start()
            for d in (0, 1):
                gather1(ref, d, u).start()
            twin(ref, 0, u).start()

        on_ref(u, send)
        for kind in (0, 1, 2):
            for d in (0, 1):
                along(kind, d, u).wait_send()

    def z4(u):
        def body(ref):
            for d in (0, 1):
                gather1(ref, d, u).wait_recv()
                gather2(ref, d, u).start()
                twin(ref, 1 + d, u).start()
            keep(ref, u).wait()
            for d in (0, 1):
                gather1(ref, d, u).wait_send()
            twin(ref, 0, u).wait_send()

        on_ref(u, body)

    def z5(u):
        def body(ref):
            for d in (0, 1):
                gather2(ref, d, u).wait_recv()
            twin(ref, 3, u).start()
            for d in (0, 1):
                gather2(ref, d, u).wait_send()
                twin(ref, 1 + d, u).wait_send()

        on_ref(u, body)

    def z6(u):
        def body(ref):
            twin(ref, 3, u).wait_send()
            for k in range(4):
                twin(ref, k, u).wait_recv()

        on_ref(u, body)

    def product(left, right, j):
        turned[...] = left.T
        at = pl.ds(pl.multiple_of((j % 3) * 256, 256), 256)

        @pl.loop(0, 8)
        def _(q):
            both = jnp.dot(
                turned[...],
                right[:, pl.ds(pl.multiple_of(q * 256, 256), 256)],
                preferred_element_type=F32,
            )
            for k in (0, 1):
                stream[q // 2, (q % 2) * 2 + k, at] = both[:, k * 128 : (k + 1) * 128]

    def block(j):
        @pl.when(j < 4)
        def _():
            product(act_ref[:, pl.ds(pl.multiple_of(j % 4 * 256, 256), 256)], g_ref, j)

        @pl.when((j >= 4) & (j < 8))
        def _():
            product(gh_ref[:, pl.ds(pl.multiple_of(j % 4 * 256, 256), 256)], n_ref, j)

        @pl.when(j == 8)
        def _():
            product(att_ref[...], g_ref, j)

        @pl.when(j > 8)
        def _():
            product(gp_ref[j - 9], n_ref, j)

    def within(i, n):
        return (i >= 0) & (i < n)

    pl.semaphore_wait(barrier, len(SIDES))

    @pl.loop(0, TICKS)
    def _(t):
        b = t - 1
        pl.when(within(t, UNITS))(lambda: z0(t))

        @pl.when(within(b, BATCHES))
        def _():
            @pl.when(b % 4 < 3)
            def _():
                block((b // 4) * 3 + b % 4)

            x0(b)

        pl.when(within(t, UNITS))(lambda: z1(t))
        pl.when(within(t - 2, BATCHES))(lambda: x1(t - 2))
        pl.when(within(t - 1, UNITS))(lambda: z2(t - 1))
        pl.when(within(t - 3, BATCHES))(lambda: x2(t - 3))
        pl.when(within(t - 2, UNITS))(lambda: z3(t - 2))
        pl.when(within(t - 4, BATCHES))(lambda: x3(t - 4))
        pl.when(within(t - 3, UNITS))(lambda: z4(t - 3))
        pl.when(within(t - 5, BATCHES))(lambda: x4(t - 5))
        pl.when(within(t - 4, UNITS))(lambda: z5(t - 4))
        pl.when(within(t - 5, UNITS))(lambda: z6(t - 5))


def run_layer(x, g, normed, act, att, gh, gp, sw, dw, ew, aw, vec):
    vmem = pl.BlockSpec(memory_space=pltpu.VMEM)
    anym = pl.BlockSpec(memory_space=pl.ANY)
    dma = pltpu.SemaphoreType.DMA
    return pl.pallas_call(
        layer_kernel,
        out_shape=(
            jax.ShapeDtypeStruct((LENGTH, D), F32),
            jax.ShapeDtypeStruct((LENGTH, D), F32),
            jax.ShapeDtypeStruct((3072, 128), F32),
            jax.ShapeDtypeStruct((8, D), F32),
        ),
        in_specs=[vmem] * 12,
        out_specs=(anym, anym, vmem, vmem),
        scratch_shapes=[
            pltpu.VMEM((4, 4, 4 * BROWS, 128), F32),
            pltpu.VMEM((256, LENGTH), BF16),
            pltpu.VMEM((2, UROWS, D), F32),
            pltpu.VMEM((2, 64, D), F32),
            pltpu.VMEM((3, 64, D), F32),
            pltpu.VMEM((2, KZ, 8, D), F32),
            pltpu.VMEM((2, KZ, 8, D), F32),
            pltpu.VMEM((2, KZ, 8, D), F32),
            pltpu.VMEM((2, 16, D), F32),
            pltpu.VMEM((2, 2, KX, 4, 48, 128), F32),
            pltpu.VMEM((2, 2, KX, 4, 48, 128), F32),
            pltpu.VMEM((2, 2, KX, 4, 48, 128), F32),
            pltpu.VMEM((2, KX, 4, 96, 128), F32),
            pltpu.VMEM((2, 2, KX, 48, 128), F32),
            pltpu.VMEM((2, 2, KX, 48, 128), F32),
            pltpu.VMEM((2, 2, KX, 48, 128), F32),
            dma((3, 2, 2, KX)),
            dma((3, 2, 2, KX)),
            dma((3, 2, 2, KX)),
            dma((3, 2, 2, KX)),
            dma((2,)),
            dma((2,)),
            dma((3, 2, KZ)),
            dma((3, 2, KZ)),
            dma((2, 2, KZ)),
            dma((2, 2, KZ)),
            dma((4, KZ)),
            dma((4, KZ)),
            dma((2,)),
        ],
        compiler_params=pltpu.CompilerParams(
            collective_id=0, has_side_effects=True, vmem_limit_bytes=62 << 20
        ),
        cost_estimate=pl.CostEstimate(flops=20 << 30, bytes_accessed=60 << 20, transcendentals=0),
    )(x, g, normed, act, att, gh, gp, sw, dw, ew, aw, vec)


def layer_norm(values, gain, shift):
    center = jnp.mean(values, axis=-1, keepdims=True)
    centred = values - center
    spread = jnp.mean(centred * centred, axis=-1, keepdims=True)
    return centred * lax.rsqrt(spread + norm_eps) * gain + shift


def gelu_tanh(values):
    return (
        0.5
        * values
        * (1.0 + jnp.tanh(0.7978845608 * (values + 0.044715 * values * values * values)))
    )


def rotary_tables(length, rot_dims):
    halfway = rot_dims // 2
    powers = jnp.arange(halfway).astype(jnp.float32) * (2.0 / rot_dims)
    freqs = jnp.exp(-powers * jnp.log(jnp.float32(rotary_base)))
    angles = jnp.arange(length).astype(jnp.float32)[:, None] * freqs[None, :]
    angles = jnp.concatenate([angles, angles], axis=1)
    return (jnp.cos(angles), jnp.sin(angles))


def rotate_heads(heads, cosine, sine, rot_dims):
    halfway = rot_dims // 2
    turned_part = heads[..., :rot_dims]
    swapped = jnp.concatenate([-turned_part[..., halfway:], turned_part[..., :halfway]], axis=-1)
    result = turned_part * cosine[:, None, :] + swapped * sine[:, None, :]
    return jnp.concatenate([result, heads[..., rot_dims:]], axis=-1)


def per_device(
    inputs,
    norm_gain,
    norm_bias,
    attn_weight,
    attn_bias,
    dense_weight,
    dense_bias,
    expand_weight,
    expand_bias,
    shrink_weight,
    shrink_bias,
    cotangent,
):
    tok_rows = inputs.shape[0]
    local_width = attn_weight.shape[2]
    local_heads = local_width // HD
    sequences = tok_rows // LENGTH
    row_block = min(512, LENGTH)
    factor = HD ** (-0.5)
    states = inputs.astype(jnp.float32)
    normed_full, norm_back = jax.vjp(
        layer_norm, states, norm_gain.astype(jnp.float32), norm_bias.astype(jnp.float32)
    )
    normed = normed_full.astype(jnp.bfloat16)
    proj = jnp.einsum("td,kde->kte", normed, attn_weight, preferred_element_type=jnp.float32)
    proj = (proj + attn_bias.astype(jnp.float32)[:, None, :]).reshape(
        3, sequences, LENGTH, local_heads, HD
    )
    cosine, sine = rotary_tables(LENGTH, ROT)

    def turn_heads(heads):
        return rotate_heads(heads, cosine, sine, ROT)

    query_full, query_back = jax.vjp(turn_heads, proj[0])
    key_full, key_back = jax.vjp(turn_heads, proj[1])
    query = query_full.astype(jnp.bfloat16)
    keys = key_full.astype(jnp.bfloat16)
    values = proj[2].astype(jnp.bfloat16)
    pieces = []
    log_totals = []
    for start_row in range(0, LENGTH, row_block):
        stop_row = start_row + row_block
        query_rows = query[:, start_row:stop_row]
        scores = (
            jnp.einsum(
                "sqhd,skhd->shqk",
                query_rows,
                keys[:, :stop_row],
                preferred_element_type=jnp.float32,
            )
            * factor
        )
        allowed = jnp.arange(stop_row)[None, :] <= (start_row + jnp.arange(row_block))[:, None]
        scores = jnp.where(allowed, scores, -1e30)
        row_top = jnp.max(scores, axis=-1, keepdims=True)
        expo = jnp.exp(scores - row_top)
        row_total = jnp.sum(expo, axis=-1, keepdims=True)
        chances = (expo / row_total).astype(jnp.bfloat16)
        pieces.append(
            jnp.einsum(
                "shqk,skhd->sqhd", chances, values[:, :stop_row], preferred_element_type=jnp.float32
            )
        )
        log_totals.append(row_top + jnp.log(row_total))
    attended = jnp.concatenate(pieces, axis=1).reshape(tok_rows, local_width).astype(jnp.bfloat16)
    hidden = jnp.dot(
        normed, expand_weight, preferred_element_type=jnp.float32
    ) + expand_bias.astype(jnp.float32)
    act_full, gelu_back = jax.vjp(gelu_tanh, hidden)
    act = act_full.astype(jnp.bfloat16)
    grad_full = cotangent.astype(jnp.float32)
    bias_term = jnp.sum(grad_full, axis=0)
    grad_act = jnp.einsum("td,fd->tf", cotangent, shrink_weight, preferred_element_type=jnp.float32)
    grad_hidden = gelu_back(grad_act)[0].astype(jnp.bfloat16)
    expand_bias_term = jnp.sum(grad_hidden.astype(jnp.float32), axis=0)
    grad_att = jnp.einsum("td,ed->te", cotangent, dense_weight, preferred_element_type=jnp.float32)
    grad_att = grad_att.astype(jnp.bfloat16).reshape(sequences, LENGTH, local_heads, HD)
    grad_query_parts = []
    grad_keys = jnp.zeros((sequences, LENGTH, local_heads, HD), jnp.float32)
    grad_values = jnp.zeros((sequences, LENGTH, local_heads, HD), jnp.float32)
    for number, start_row in enumerate(range(0, LENGTH, row_block)):
        stop_row = start_row + row_block
        query_rows = query[:, start_row:stop_row]
        key_rows = keys[:, :stop_row]
        value_rows = values[:, :stop_row]
        grad_rows = grad_att[:, start_row:stop_row]
        scores = (
            jnp.einsum("sqhd,skhd->shqk", query_rows, key_rows, preferred_element_type=jnp.float32)
            * factor
        )
        allowed = jnp.arange(stop_row)[None, :] <= (start_row + jnp.arange(row_block))[:, None]
        chances = jnp.where(allowed, jnp.exp(scores - log_totals[number]), 0.0)
        grad_chances = jnp.einsum(
            "sqhd,skhd->shqk", grad_rows, value_rows, preferred_element_type=jnp.float32
        )
        row_dot = jnp.sum(chances * grad_chances, axis=-1, keepdims=True)
        grad_scores = (chances * (grad_chances - row_dot)).astype(jnp.bfloat16)
        grad_query_parts.append(
            jnp.einsum("shqk,skhd->sqhd", grad_scores, key_rows, preferred_element_type=jnp.float32)
            * factor
        )
        padding = ((0, 0), (0, LENGTH - stop_row), (0, 0), (0, 0))
        grad_keys = grad_keys + jnp.pad(
            jnp.einsum(
                "shqk,sqhd->skhd", grad_scores, query_rows, preferred_element_type=jnp.float32
            )
            * factor,
            padding,
        )
        grad_values = grad_values + jnp.pad(
            jnp.einsum(
                "shqk,sqhd->skhd",
                chances.astype(jnp.bfloat16),
                grad_rows,
                preferred_element_type=jnp.float32,
            ),
            padding,
        )
    grad_query_pre = query_back(jnp.concatenate(grad_query_parts, axis=1))[0]
    grad_key_pre = key_back(grad_keys)[0]
    grad_proj = (
        jnp.stack([grad_query_pre, grad_key_pre, grad_values])
        .reshape(3, tok_rows, local_width)
        .astype(jnp.bfloat16)
    )
    attn_bias_term = jnp.sum(grad_proj.astype(jnp.float32), axis=1)
    vec = jnp.concatenate(
        [
            norm_gain.astype(F32)[None],
            (dense_bias.astype(F32) + shrink_bias.astype(F32))[None],
            jnp.zeros((6, D), F32),
        ]
    )
    summed, input_grad, pieces, sums = run_layer(
        inputs, cotangent, normed, act, attended, grad_hidden, grad_proj,
        shrink_weight, dense_weight, expand_weight, attn_weight, vec,
    )
    output = summed.astype(BF16)
    shrink_sum = pieces[:1024]
    expand_sum = pieces[1024:2048].T
    dense_sum = pieces[2048:2304]
    attn_sum = jnp.swapaxes(pieces[2304:].reshape(3, 256, 128), 1, 2)
    both = lax.psum(sums[:2], "tensor")
    gain_sum, shift_sum, bias_sum = lax.psum_scatter(
        jnp.concatenate([both, bias_term[None]]), "dp", scatter_dimension=1, tiled=True
    )
    attn_bias_sum = lax.psum_scatter(attn_bias_term, "dp", scatter_dimension=1, tiled=True)
    expand_bias_sum = lax.psum_scatter(expand_bias_term, "dp", scatter_dimension=0, tiled=True)
    return (
        output, input_grad, gain_sum, shift_sum, attn_sum, attn_bias_sum, dense_sum, bias_sum,
        expand_sum, expand_bias_sum, shrink_sum, bias_sum,
    )


def solution(mesh):
    placed = (
        P("dp", None),
        P(),
        P(),
        P(None, None, "tensor"),
        P(None, "tensor"),
        P("tensor", None),
        P(),
        P(None, "tensor"),
        P("tensor"),
        P("tensor", None),
        P(),
        P("dp", None),
    )
    return jax.shard_map(
        per_device,
        mesh=mesh,
        in_specs=placed,
        out_specs=(
            P("dp", None),
            P("dp", None),
            P("dp"),
            P("dp"),
            P(None, "dp", "tensor"),
            P(None, ("tensor", "dp")),
            P("tensor", "dp"),
            P("dp"),
            P("dp", "tensor"),
            P(("tensor", "dp")),
            P("tensor", "dp"),
            P("dp"),
        ),
        check_vma=False,
    )
```

```python
import jax
import jax.numpy as jnp
import numpy as np
from jax import lax
from jax.experimental import pallas as pl
from jax.experimental.pallas import tpu as pltpu
from jax.sharding import PartitionSpec as P

HD = 64
ROT = 32
LENGTH = 1024
D = 2048
F32 = jnp.float32
BF16 = jnp.bfloat16
MESH = pl.DeviceIdType.MESH

rotary_base = 10000.0
norm_eps = 1e-05

CH = 256
UNITS = 16
UROWS = 128
BATCHES = 16
BROWS = 192
KX = 5
KY = 5
KZ = 5
KT = 8
KG = 4
TICKS = 23


def gelu_parts(v):
    th = jnp.tanh(0.7978845608 * (v + 0.044715 * v * v * v))
    return th, 0.5 * (1.0 + th)


def layer_kernel(
    x_hbm, g_hbm, sw_hbm, dw_hbm, ew_hbm, aw_hbm, cos_hbm, sin_hbm, gain_hbm, shift_hbm, eb_hbm, ab_hbm, db_hbm, sb_hbm,
    all_ref, f_ref, small_ref,
    vec_ref, gain_ref, shift_ref, eb_ref, ab_ref, db_ref, sb_ref, xo_ref, g_ref, n_ref, act_ref, att_ref, gh_ref, gp_ref, q_ref, k_ref, v_ref, ga_ref,
    st_ref, top_ref, sum_ref, dq_ref, dk_ref, dv_ref, km_ref, qm_ref, gm_ref, pm_ref, dl_ref, ds_ref, cos_ref, sin_ref, sw_ref, dw_ref, ew_ref, aw_ref, gs_ref,
    va, vb, vc, vd, ve,
    stream, turned, part, core_in, mine, zp, zd, zb, zg, done,
    xp, xd, xb, mid, yp, yd, yb,
    xsend, xrecv, ysend, yrecv, csend, crecv, zsend, zrecv, gsend, grecv, ssend, srecv, lsem,
    isem, osem, vsend, vrecv,
):
    dp = lax.axis_index("dp")
    tn = lax.axis_index("tensor")
    x, y, c, z = dp % 4, dp // 4, tn % 2, tn // 2

    def side(axis, sg):
        if axis == 0:
            return (y * 4 + (x + sg + 4) % 4, tn)
        if axis == 1:
            return (((y + sg + 4) % 4) * 4 + x, tn)
        if axis == 2:
            return (dp, ((z + sg + 4) % 4) * 2 + c)
        return (dp, z * 2 + 1 - c)

    def load(k):
        rows = pl.ds((k % 4) * CH, CH)
        src, dst = (
            (x_hbm.at[rows], n_ref.at[rows])
            if k < 4
            else (g_hbm.at[rows], g_ref.at[rows])
            if k < 8
            else (
                (sw_hbm, sw_ref),
                (dw_hbm, dw_ref),
                (ew_hbm, ew_ref),
                (aw_hbm, aw_ref),
                (cos_hbm, cos_ref),
                (sin_hbm, sin_ref),
                (gain_hbm, gain_ref),
                (shift_hbm, shift_ref),
                (db_hbm, db_ref),
                (sb_hbm, sb_ref),
                (eb_hbm, eb_ref),
                (ab_hbm, ab_ref),
            )[k - 8]
        )
        return pltpu.make_async_copy(src, dst, isem.at[k])

    for k in (0, 14, 15, 16, 17, 18, 19, 10, 11):
        load(k).start()

    SIDES = [(0, 1), (0, -1), (0, 2), (1, 1), (1, -1), (1, 2), (2, 1), (2, -1), (2, 2), (3, 0)]
    barrier = pltpu.get_barrier_semaphore()
    for axis, sg in SIDES:
        pl.semaphore_signal(barrier, inc=1, device_id=side(axis, sg), device_id_type=MESH)

    gs_ref[...] = jnp.zeros_like(gs_ref)

    def remote(src, dst, ssem, rsem, to):
        return pltpu.make_async_remote_copy(
            src_ref=src, dst_ref=dst, send_sem=ssem, recv_sem=rsem, device_id=to, device_id_type=MESH
        )

    def within(i, n):
        return (i >= 0) & (i < n)

    def when(cond, body, *args):
        pl.when(cond)(lambda: body(*args))

    NT = (((1,), (1,)), ((), ()))
    SG = (1, -1)
    HALVES = (0, 1)

    def rows_of(b, h, hh):
        return pl.ds(pl.multiple_of((b % 4) * BROWS + h * 96 + hh * 48, 8), 48)

    def own_rows(b, h, piece, hh):
        return (
            stream.at[:, piece, rows_of(b, h, hh)]
            if h == 0
            else stream.at[piece, :, rows_of(b, h, hh)]
        )

    def first(kind, h, d, b):
        a = (x, y)[h]
        sg = SG[d]
        slot = b % KX
        sems = (xsend.at[kind, h, d, slot], xrecv.at[kind, h, d, slot], side(h, sg))
        if kind == 0:
            return remote(own_rows(b, h, (a + 2) % 4, d), xp.at[h, d, slot], *sems)
        if kind == 1:
            return remote(own_rows(b, h, (a + sg + 4) % 4, 1 - d), xd.at[h, d, slot], *sems)
        return remote(xp.at[h, d, slot], xb.at[h, d, slot], *sems)

    def second(kind, h, d, b):
        a = (y, x)[h]
        sg = SG[d]
        slot = b % KY
        sems = (ysend.at[kind, h, d, slot], yrecv.at[kind, h, d, slot], side(1 - h, sg))
        if kind == 0:
            return remote(mid.at[h, b % 3, (a + 2) % 4, pl.ds(d * 48, 48)], yp.at[h, d, slot], *sems)
        if kind == 1:
            return remote(
                mid.at[h, b % 3, (a + sg + 4) % 4, pl.ds((1 - d) * 48, 48)], yd.at[h, d, slot], *sems
            )
        return remote(yp.at[h, d, slot], yb.at[h, d, slot], *sems)

    def each(make, kinds, b):
        for kind in kinds:
            for h in HALVES:
                for d in (0, 1):
                    yield make(kind, h, d, b)

    def x0(b):
        for copy in each(first, (0, 1), b):
            copy.start()

    def x1(b):
        slot = b % KX
        for h in HALVES:
            for d in (0, 1):
                a = (x, y)[h]
                first(0, h, d, b).wait_recv()
                xp[h, d, slot] = xp[h, d, slot] + own_rows(b, h, (a + SG[d] + 4) % 4, d)[...]
                first(2, h, d, b).start()

    def x2(b):
        slot = b % KX
        for h in HALVES:
            a = (x, y)[h]
            for d in (0, 1):
                first(1, h, d, b).wait_recv()
                first(2, h, d, b).wait_recv()
            for hh in (0, 1):
                mid[h, b % 3, :, pl.ds(hh * 48, 48)] = (
                    own_rows(b, h, a, hh)[...] + xb[h, hh, slot] + xd[h, 1 - hh, slot]
                )
            for kind in (0, 1):
                for d in (0, 1):
                    second(kind, h, d, b).start()
        for copy in each(first, (0, 1, 2), b):
            copy.wait_send()

    def x3(b):
        slot = b % KY
        for h in HALVES:
            a = (y, x)[h]
            for d in (0, 1):
                second(0, h, d, b).wait_recv()
                yp[h, d, slot] = (
                    yp[h, d, slot] + mid[h, b % 3, (a + SG[d] + 4) % 4, pl.ds(d * 48, 48)]
                )
                second(2, h, d, b).start()

    def x4(b):
        slot = b % KY
        for h in HALVES:
            a = (y, x)[h]
            for d in (0, 1):
                second(1, h, d, b).wait_recv()
                second(2, h, d, b).wait_recv()
            for hh in (0, 1):
                at = pl.ds(pl.multiple_of(b * BROWS + h * 96 + hh * 48, 8), 48)
                f_ref[at] = mid[h, b % 3, a, pl.ds(hh * 48, 48)] + yb[h, hh, slot] + yd[h, 1 - hh, slot]
        for copy in each(second, (0, 1, 2), b):
            copy.wait_send()

    def zrows(u, piece, hh):
        return mine.at[u % 3, pl.ds(pl.multiple_of(piece * 16 + hh * 8, 8), 8)]

    def along(kind, d, u):
        sg = SG[d]
        slot = u % KZ
        sems = (zsend.at[kind, d, slot], zrecv.at[kind, d, slot], side(2, sg))
        if kind == 0:
            return remote(zrows(u, (z + 2) % 4, d), zp.at[d, slot], *sems)
        if kind == 1:
            return remote(zrows(u, (z + sg + 4) % 4, 1 - d), zd.at[d, slot], *sems)
        return remote(zp.at[d, slot], zb.at[d, slot], *sems)

    def cross(u):
        return remote(
            part.at[u % 2, pl.ds(pl.multiple_of((1 - c) * 64, 64), 64)],
            core_in.at[u % 2],
            csend.at[u % 2],
            crecv.at[u % 2],
            side(3, 0),
        )

    def grow(u, cc, piece, off, size):
        return pl.ds(pl.multiple_of((u % 8) * UROWS + cc * 64 + piece * 16 + off, 8), size)

    def gather1(d, u):
        slot = u % KZ
        return remote(
            done.at[u % 2], zg.at[u % KG, d], gsend.at[0, d, slot], grecv.at[0, d, slot],
            side(2, SG[d]),
        )

    def gather2(d, u):
        slot = u % KZ
        half = pl.ds(d * 8, 8)
        return remote(
            zg.at[u % KG, d, half], zg.at[u % KG, 2, half], gsend.at[1, d, slot],
            grecv.at[1, d, slot], side(2, SG[d]),
        )

    def block_rows(k, u):
        return all_ref.at[u // 8, grow(u, c, (z + (0, -1, 1, 2)[k] + 4) % 4, 0, 16)]

    def block_held(k, u):
        return done.at[u % 2] if k == 0 else zg.at[u % KG, k - 1]

    def twin(k, u):
        slot = u % KT
        return remote(
            block_held(k, u), block_rows(k, u), ssend.at[k, slot], srecv.at[k, slot], side(3, 0)
        )

    def keep(k, u):
        return pltpu.make_async_copy(block_held(k, u), block_rows(k, u), lsem.at[k, u % KG])

    def partial(u, j):
        rows = pl.ds(pl.multiple_of((u % 8) * UROWS, CH), CH)
        cols = pl.ds(pl.multiple_of(j * 1024, 1024), 1024)

        def put(total):
            part[0, :, cols] = total[:UROWS]
            part[1, :, cols] = total[UROWS:]

        @pl.when(u < 8)
        def _():
            put(
                jnp.dot(act_ref[rows, :], sw_ref[:, cols], preferred_element_type=F32)
                + jnp.dot(att_ref[rows, :], dw_ref[:, cols], preferred_element_type=F32)
            )

        @pl.when(u >= 8)
        def _():
            total = lax.dot_general(
                gh_ref[rows, :], ew_ref[cols, :], NT, preferred_element_type=F32
            )
            for k in range(3):
                total += lax.dot_general(
                    gp_ref[k, rows, :], aw_ref[k, cols, :], NT, preferred_element_type=F32
                )
            put(total)

    def z1(u):
        cross(u).wait_recv()

        @pl.loop(0, 2)
        def _(k):
            at = pl.ds(pl.multiple_of(k * 32, 32), 32)
            mine[u % 3, at] = (
                part[u % 2, pl.ds(pl.multiple_of(c * 64 + k * 32, 32), 32)] + core_in[u % 2, at]
            )

        for kind in (0, 1):
            for d in (0, 1):
                along(kind, d, u).start()
        cross(u).wait_send()

    def own_x(u):
        rows = pl.ds(pl.multiple_of((u % 8) * UROWS + c * 64 + z * 16, 16), 16)
        return pltpu.make_async_copy(x_hbm.at[rows], xo_ref.at[u % 2], osem.at[u % 2])

    def z2(u):
        slot = u % KZ
        own_x(u).start()
        for d in (0, 1):
            along(0, d, u).wait_recv()
            zp[d, slot] = zp[d, slot] + zrows(u, (z + SG[d] + 4) % 4, d)[...]
            along(2, d, u).start()

    def z3(u):
        slot = u % KZ
        for d in (0, 1):
            along(1, d, u).wait_recv()
            along(2, d, u).wait_recv()
        whole = jnp.concatenate(
            [zrows(u, z, hh)[...] + zb[hh, slot] + zd[1 - hh, slot] for hh in (0, 1)], axis=0
        )
        rows = pl.ds(pl.multiple_of((u % 8) * UROWS + c * 64 + z * 16, 16), 16)
        own_x(u).wait()
        states = xo_ref[u % 2].astype(F32)

        @pl.when(u < 8)
        def _():
            done[u % 2] = states + whole + vec_ref[2:3, :]

        @pl.when(u >= 8)
        def _():
            center = jnp.mean(states, axis=-1, keepdims=True)
            centred = states - center
            spread = jnp.mean(centred * centred, axis=-1, keepdims=True)
            r = lax.rsqrt(spread + norm_eps)
            zz = centred * r
            e = whole * vec_ref[0:1, :]
            done[u % 2] = g_ref[rows, :].astype(F32) + r * (
                e
                - jnp.mean(e, axis=-1, keepdims=True)
                - zz * jnp.mean(e * zz, axis=-1, keepdims=True)
            )
            gs_ref[0:1, :] += jnp.sum(whole * zz, axis=0, keepdims=True)
            gs_ref[1:2, :] += jnp.sum(whole, axis=0, keepdims=True)

        for d in (0, 1):
            gather1(d, u).start()
        twin(0, u).start()
        keep(0, u).start()
        for kind in (0, 1, 2):
            for d in (0, 1):
                along(kind, d, u).wait_send()

    def z4(u):
        for d in (0, 1):
            gather1(d, u).wait_recv()
        for d in (0, 1):
            gather2(d, u).start()
        for d in (0, 1):
            twin(1 + d, u).start()
            keep(1 + d, u).start()
        keep(0, u).wait()
        for d in (0, 1):
            gather1(d, u).wait_send()
        twin(0, u).wait_send()

    def z5(u):
        for d in (0, 1):
            gather2(d, u).wait_recv()
        twin(3, u).start()
        keep(3, u).start()
        for d in (0, 1):
            gather2(d, u).wait_send()
            twin(1 + d, u).wait_send()
            keep(1 + d, u).wait()

    def z6(u):
        twin(3, u).wait_send()
        keep(3, u).wait()
        for k in range(4):
            twin(k, u).wait_recv()

    def product(left, right, j, q):
        @pl.when(q == 0)
        def _():
            turned[...] = left[...].T

        at = pl.ds(pl.multiple_of((j % 3) * 256, 256), 256)
        both = jnp.dot(
            turned[...],
            right[:, pl.ds(pl.multiple_of(q * 1024, 1024), 1024)],
            preferred_element_type=F32,
        )
        for k in range(8):
            stream[q * 2 + k // 4, k % 4, at] = both[:, k * 128 : (k + 1) * 128]

    def block(j, q):
        cols = pl.ds(pl.multiple_of(j % 4 * 256, 256), 256)
        when(j < 4, product, act_ref.at[:, cols], g_ref, j, q)
        when((j >= 4) & (j < 8), product, gh_ref.at[:, cols], n_ref, j, q)
        when(j == 8, product, att_ref, g_ref, j, q)
        when(j > 8, product, gp_ref.at[jnp.maximum(j - 9, 0)], n_ref, j, q)

    lane = lax.broadcasted_iota(jnp.int32, (1, 256), 1)

    def chunk(i):
        return pl.ds(pl.multiple_of(i * CH, CH), CH)

    def norm_chunk(i):
        @pl.loop(0, 2)
        def _(k):
            rows = pl.ds(pl.multiple_of(i * CH + k * 128, 128), 128)
            states = n_ref[rows, :].astype(F32)
            centred = states - jnp.mean(states, axis=-1, keepdims=True)
            spread = jnp.mean(centred * centred, axis=-1, keepdims=True)
            n_ref[rows, :] = (
                centred * lax.rsqrt(spread + norm_eps) * vec_ref[0:1, :] + vec_ref[1:2, :]
            ).astype(BF16)

    def expand_part(rows, j):
        cols = pl.ds(pl.multiple_of(j * 256, 256), 256)
        hidden = (
            jnp.dot(n_ref[rows, :], ew_ref[:, cols], preferred_element_type=F32)
            + vec_ref[3:4, cols]
        )
        th, half = gelu_parts(hidden)
        act_ref[rows, cols] = (hidden * half).astype(BF16)
        gh_ref[rows, cols] = (
            half
            + (0.5 * 0.7978845608) * hidden * (1.0 - th * th) * (
                1.0 + (3 * 0.044715) * hidden * hidden
            )
        ).astype(BF16)

    def hidden_back(j):
        cols = pl.ds(pl.multiple_of(j * 256, 256), 256)
        back = lax.dot_general(g_ref[...], sw_ref[cols, :], NT, preferred_element_type=F32)
        gh_ref[:, cols] = (back * gh_ref[:, cols].astype(F32)).astype(BF16)

    def turn(values, i, way):
        cosine = cos_ref[chunk(i), :]
        sine = sin_ref[chunk(i), :] * way
        low = lax.broadcasted_iota(jnp.int32, (1, 128), 1) % HD < ROT // 2
        halves = []
        for k in (0, 1):
            v = values[:, k * 128 : (k + 1) * 128]
            swapped = jnp.where(low, -pltpu.roll(v, 128 - ROT // 2, 1), pltpu.roll(v, ROT // 2, 1))
            halves.append(v * cosine + swapped * sine)
        return jnp.concatenate(halves, axis=1)

    def project_chunk(i):
        rows = chunk(i)

        def proj(k):
            return (
                jnp.dot(n_ref[rows, :], aw_ref[k], preferred_element_type=F32)
                + vec_ref[4:5, k * 256 : (k + 1) * 256]
            )

        q_ref[rows, :] = (turn(proj(0), i, 1.0).astype(BF16).astype(F32) * HD**-0.5).astype(BF16)
        k_ref[rows, :] = turn(proj(1), i, 1.0).astype(BF16)
        v_ref[rows, :] = proj(2).astype(BF16)
        ga_ref[rows, :] = lax.dot_general(
            g_ref[rows, :], dw_ref[...], NT, preferred_element_type=F32
        ).astype(BF16)

    HEADS = [slice(h * CH, (h + 1) * CH) for h in range(4)]
    high = lax.broadcasted_iota(jnp.int32, (256, 1), 0)

    def stack_heads(out, values):
        for h in range(4):
            out[HEADS[h], :] = jnp.where(lane // HD == h, values, 0)

    def scores_of(i, j, h, scores):
        allowed = j * CH + lax.broadcasted_iota(
            jnp.int32, (CH, CH), 0
        ) <= i * CH + lax.broadcasted_iota(jnp.int32, (CH, CH), 1)
        return jnp.where(allowed, scores[:, HEADS[h]], -1e30)

    def scores_pair(i, j):
        return lax.dot_general(k_ref[chunk(j), :], qm_ref[...], NT, preferred_element_type=F32)

    def attend_begin(i):
        stack_heads(qm_ref, q_ref[chunk(i), :])
        top_ref[...] = jnp.full_like(top_ref, -1e30)
        sum_ref[...] = jnp.zeros_like(sum_ref)
        dk_ref[...] = jnp.zeros_like(dk_ref)

    def attend_pair(i, j):
        rows = chunk(i)
        scores = scores_pair(i, j)
        values_turned = v_ref[chunk(j), :].T
        for h in range(4):
            part_scores = scores_of(i, j, h, scores)
            old = top_ref[h : h + 1, :]
            top = jnp.maximum(old, jnp.max(part_scores, axis=0, keepdims=True))
            less = jnp.exp(old - top)
            expo = jnp.exp(part_scores - top)
            sum_ref[h : h + 1, :] = sum_ref[h : h + 1, :] * less + jnp.sum(
                expo, axis=0, keepdims=True
            )
            top_ref[h : h + 1, :] = top
            km_ref[:, HEADS[h]] = jnp.where(high // HD == h, values_turned, 0)
            ds_ref[HEADS[h], :] = expo.astype(BF16)
            dk_ref[h * HD : (h + 1) * HD, :] = dk_ref[h * HD : (h + 1) * HD, :] * less
        dk_ref[...] += jnp.dot(km_ref[...], ds_ref[...], preferred_element_type=F32)

        @pl.when(j == i)
        def _():
            for h in range(4):
                at = slice(h * HD, (h + 1) * HD)
                dk_ref[at, :] = dk_ref[at, :] * (1.0 / sum_ref[h : h + 1, :])
            st_ref[0:4, rows] = top_ref[0:4, :] + jnp.log(sum_ref[0:4, :])
            total = dk_ref[...]
            att_ref[rows, :] = total.T.astype(BF16)
            dots = total * ga_ref[rows, :].astype(F32).T
            for h in range(4):
                st_ref[4 + h : 5 + h, rows] = jnp.sum(
                    dots[h * HD : (h + 1) * HD], axis=0, keepdims=True
                )

    def attend_back(j, i):
        rows = chunk(j)
        qrows = chunk(i)
        key = k_ref[rows, :]

        @pl.when(i == j)
        def _():
            keys_turned = key.T
            for h in range(4):
                km_ref[:, HEADS[h]] = jnp.where(high // HD == h, keys_turned, 0)
            dk_ref[...] = jnp.zeros_like(dk_ref)
            dv_ref[...] = jnp.zeros_like(dv_ref)

        stack_heads(qm_ref, q_ref[qrows, :])
        stack_heads(gm_ref, ga_ref[qrows, :])
        scores = lax.dot_general(key, qm_ref[...], NT, preferred_element_type=F32)
        back = lax.dot_general(v_ref[rows, :], gm_ref[...], NT, preferred_element_type=F32)
        for h in range(4):
            chances = jnp.exp(scores_of(i, j, h, scores) - st_ref[h : h + 1, qrows])
            dscore = (chances * (back[:, HEADS[h]] - st_ref[4 + h : 5 + h, qrows])).astype(BF16)
            pm_ref[:, HEADS[h]] = chances.astype(BF16)
            dl_ref[:, HEADS[h]] = dscore
            ds_ref[HEADS[h], :] = dscore
        dk_ref[...] += jnp.dot(dl_ref[...], qm_ref[...], preferred_element_type=F32)
        dv_ref[...] += jnp.dot(pm_ref[...], gm_ref[...], preferred_element_type=F32)
        dq_ref[:, qrows] += jnp.dot(km_ref[...], ds_ref[...], preferred_element_type=F32)

        @pl.when(i == 3)
        def _():
            gp_ref[0, rows, :] = turn(dq_ref[:, rows].T * HD**-0.5, j, -1.0).astype(BF16)
            gp_ref[1, rows, :] = turn(dk_ref[...], j, -1.0).astype(BF16)
            gp_ref[2, rows, :] = dv_ref[...].astype(BF16)

    def token_sums():
        ones = jnp.ones((8, LENGTH), BF16)
        sums = jnp.dot(ones, g_ref[...], preferred_element_type=F32)
        hsum = jnp.dot(ones, gh_ref[...], preferred_element_type=F32)
        psum = [jnp.dot(ones, gp_ref[k], preferred_element_type=F32) for k in range(3)]
        for p in range(16):
            vc[p // 4, p % 4, 2:3] = sums[0:1, p * 128 : (p + 1) * 128]
            vc[p // 4, p % 4, 3:4] = hsum[0:1, p // 2 * 128 : (p // 2 + 1) * 128]
            for k in range(3):
                vc[p // 4, p % 4, 4 + k : 5 + k] = psum[k][0:1, p // 8 * 128 : (p // 8 + 1) * 128]
            vc[p // 4, p % 4, 7:8] = jnp.zeros((1, 128), F32)

    def v_core():
        return remote(va, vb.at[3], vsend.at[0], vrecv.at[0], side(3, 0))

    def v_z(k):
        return remote(va, vb.at[k], vsend.at[1 + k], vrecv.at[1 + k], side(2, (1, -1, 2)[k]))

    def v_x(k):
        sg = (1, -1, 2)[k]
        return remote(vc.at[:, (x + sg + 4) % 4], vd.at[k], vsend.at[4 + k], vrecv.at[4 + k], side(0, sg))

    def v_y(k):
        sg = (1, -1, 2)[k]
        return remote(vd.at[3, (y + sg + 4) % 4], ve.at[k], vsend.at[7 + k], vrecv.at[7 + k], side(1, sg))

    def v0():
        for p in range(16):
            va[p : p + 1] = gs_ref[0:1, p * 128 : (p + 1) * 128]
            va[16 + p : 17 + p] = gs_ref[1:2, p * 128 : (p + 1) * 128]
        v_core().start()

    def v1():
        v_core().wait()
        va[...] = va[...] + vb[3]
        for k in range(3):
            v_z(k).start()

    def v2():
        for k in range(3):
            v_z(k).wait()
        both = va[...] + vb[0] + vb[1] + vb[2]
        for p in range(16):
            vc[p // 4, p % 4, 0:1] = both[p : p + 1]
            vc[p // 4, p % 4, 1:2] = both[16 + p : 17 + p]
        for k in range(3):
            v_x(k).start()

    def v3():
        for k in range(3):
            v_x(k).wait()
        vd[3] = vc[:, x] + vd[0] + vd[1] + vd[2]
        for k in range(3):
            v_y(k).start()

    def v4():
        for k in range(3):
            v_y(k).wait()
        total = vd[3, y] + ve[0] + ve[1] + ve[2]
        small_ref[...] = total
        small_ref[3:4, 0:64] = jnp.where(dp % 2 == 0, total[3:4, 0:64], total[3:4, 64:128])
        mine_of = jnp.zeros((3, 16), F32)
        for k in range(8):
            mine_of = jnp.where(dp % 8 == k, total[4:7, k * 16 : (k + 1) * 16], mine_of)
        small_ref[4:7, 0:16] = mine_of

    def attend_item(k):
        i = at_least(k, 2) + at_least(k, 5) + at_least(k, 9)
        r = k - i * (i + 3) // 2

        @pl.when(r == 0)
        def _():
            project_chunk(i)
            attend_begin(i)

        when(r > 0, attend_pair, i, r - 1)

    def back_item(k):
        j = at_least(k, 4) + at_least(k, 7) + at_least(k, 9)
        attend_back(j, j + k - j * (9 - j) // 2)

    def at_least(k, bound):
        return jnp.where(k >= bound, 1, 0)

    def between(h, first, last):
        return (h >= first) & (h <= last)

    def stage(t, late, body):
        when((t >= late) & (t < late + 16), body, t - late)

    dq_ref[...] = jnp.zeros_like(dq_ref)
    for k in range(14, 20):
        load(k).wait()
    vec_ref[0:1, :] = gain_ref[...].astype(F32).reshape(1, D)
    vec_ref[1:2, :] = shift_ref[...].astype(F32).reshape(1, D)
    vec_ref[2:3, :] = (db_ref[...].astype(F32) + sb_ref[...].astype(F32)).reshape(1, D)
    vec_ref[3:4, 0:1024] = eb_ref[...].astype(F32).reshape(1, 1024)
    for k in range(3):
        vec_ref[4:5, k * 256 : (k + 1) * 256] = ab_ref[k : k + 1, :].astype(F32)
    pl.semaphore_wait(barrier, len(SIDES))

    @pl.loop(0, TICKS)
    def _(t):
        @pl.loop(0, 4)
        def _(pos):
            h = t * 4 + pos

            @pl.when(pos == 0)
            def _():
                stage(t, 6, z5)
                stage(t, 1, z1)
                stage(t, 7, x4)
                stage(t, 2, x0)
                when(t == 19, v1)
                when(t == 20, v3)

            @pl.when(pos == 1)
            def _():
                stage(t, 7, z6)
                stage(t, 2, z2)
                stage(t, 3, x1)

            @pl.when(pos == 2)
            def _():
                stage(t, 3, z3)
                stage(t, 4, x2)
                when(t == 18, v0)
                when(t == 19, v2)
                when(t == 20, v4)

            @pl.when(pos == 3)
            def _():
                stage(t, 4, z4)
                stage(t, 5, x3)

            @pl.when(t < UNITS)
            def _():
                when((pos > 0) & (pos < 3) & (t % 2 == 0), partial, t, pos - 1)
                when(pos == 2, lambda: cross(t).start())
                w = t - 1
                when(
                    (pos >= 2) & (w >= 0) & (w % 4 < 3),
                    lambda: block(w // 4 * 3 + w % 4, pos - 2),
                )

                @pl.when(h < 4)
                def _():
                    @pl.when(h == 0)
                    def _():
                        load(0).wait()
                        for k in (12, 13, 4, 9, 8):
                            load(k).start()

                    for k in range(1, 4):
                        when(h == k, load(k).wait)
                    norm_chunk(h)

                @pl.when(h == 0)
                def _():
                    load(10).wait()
                    pl.loop(0, 4)(lambda j: expand_part(pl.ds(0, CH), j))
                    for k in (1, 2, 3, 5, 6, 7):
                        load(k).start()
                    for k in (4, 9, 11, 12, 13):
                        load(k).wait()

                @pl.when(h == 3)
                def _():
                    for k in (5, 6, 7):
                        load(k).wait()

                first = jnp.where(h <= 3, 0, jnp.where(h <= 5, 1, 3))
                pl.loop(
                    first,
                    first + jnp.where(h == 5, 2, jnp.where((h == 3) | (h == 7), 1, 0)),
                )(lambda j: expand_part(pl.ds(CH, LENGTH - CH), j))
                first = jnp.where(h <= 2, 0, jnp.where(h == 3, 2, jnp.where(h <= 4, 4, h - 2)))
                pl.loop(
                    first,
                    first
                    + jnp.where(
                        (h == 0) | (h == 3), 2, jnp.where((h == 4) | between(h, 7, 15), 1, 0)
                    ),
                )(attend_item)
                when(between(h, 18, 19) | between(h, 23, 24), hidden_back, jnp.where(h < 20, h - 18, h - 21))
                back = jnp.where(
                    h <= 30, h - 27, jnp.where(h <= 36, h - 30, jnp.where(h <= 43, h - 35, 9))
                )
                when(
                    between(h, 27, 30) | between(h, 34, 36) | between(h, 42, 43) | (h == 53),
                    back_item,
                    back,
                )
                when(h == 54, token_sums)
                when(h == 0, load(8).wait)


def rotary_tables():
    freqs = np.exp(
        -np.arange(ROT // 2).astype(np.float32) * np.float32(2.0 / ROT) * np.log(np.float32(rotary_base))
    ).astype(np.float32)
    angles = np.arange(LENGTH).astype(np.float32)[:, None] * freqs[None, :]
    rest = np.zeros((LENGTH, HD - ROT), np.float32)
    one = np.concatenate([np.cos(angles), np.cos(angles), rest + 1], axis=1)
    two = np.concatenate([np.sin(angles), np.sin(angles), rest], axis=1)
    return (
        np.tile(one, (1, 2)).astype(np.float32),
        np.tile(two, (1, 2)).astype(np.float32),
    )


def run_layer(x, g, sw, dw, ew, aw, *vectors):
    vmem = pl.BlockSpec(memory_space=pltpu.VMEM)
    anym = pl.BlockSpec(memory_space=pl.ANY)
    dma = pltpu.SemaphoreType.DMA
    cosine, sine = rotary_tables()
    return pl.pallas_call(
        layer_kernel,
        out_shape=(
            jax.ShapeDtypeStruct((2, LENGTH, D), F32),
            jax.ShapeDtypeStruct((3072, 128), F32),
            jax.ShapeDtypeStruct((8, 128), F32),
        ),
        in_specs=[anym] * 14,
        out_specs=(anym, vmem, vmem),
        scratch_shapes=[
            pltpu.VMEM((8, D), F32),
            pltpu.VMEM((D,), BF16),
            pltpu.VMEM((D,), BF16),
            pltpu.VMEM((1024,), BF16),
            pltpu.VMEM((3, 256), BF16),
            pltpu.VMEM((D,), BF16),
            pltpu.VMEM((D,), BF16),
            pltpu.VMEM((2, 16, D), BF16),
            pltpu.VMEM((LENGTH, D), BF16),
            pltpu.VMEM((LENGTH, D), BF16),
            pltpu.VMEM((LENGTH, 1024), BF16),
            pltpu.VMEM((LENGTH, 256), BF16),
            pltpu.VMEM((LENGTH, 1024), BF16),
            pltpu.VMEM((3, LENGTH, 256), BF16),
            pltpu.VMEM((LENGTH, 256), BF16),
            pltpu.VMEM((LENGTH, 256), BF16),
            pltpu.VMEM((LENGTH, 256), BF16),
            pltpu.VMEM((LENGTH, 256), BF16),
            pltpu.VMEM((8, LENGTH), F32),
            pltpu.VMEM((8, CH), F32),
            pltpu.VMEM((8, CH), F32),
            pltpu.VMEM((256, LENGTH), F32),
            pltpu.VMEM((CH, 256), F32),
            pltpu.VMEM((CH, 256), F32),
            pltpu.VMEM((256, 4 * CH), BF16),
            pltpu.VMEM((4 * CH, 256), BF16),
            pltpu.VMEM((4 * CH, 256), BF16),
            pltpu.VMEM((CH, 4 * CH), BF16),
            pltpu.VMEM((CH, 4 * CH), BF16),
            pltpu.VMEM((4 * CH, CH), BF16),
            pltpu.VMEM((LENGTH, 128), F32),
            pltpu.VMEM((LENGTH, 128), F32),
            pltpu.VMEM((1024, D), BF16),
            pltpu.VMEM((256, D), BF16),
            pltpu.VMEM((D, 1024), BF16),
            pltpu.VMEM((3, D, 256), BF16),
            pltpu.VMEM((8, D), F32),
            pltpu.VMEM((32, 128), F32),
            pltpu.VMEM((4, 32, 128), F32),
            pltpu.VMEM((4, 4, 8, 128), F32),
            pltpu.VMEM((4, 4, 8, 128), F32),
            pltpu.VMEM((3, 8, 128), F32),
            pltpu.VMEM((4, 4, 4 * BROWS, 128), F32),
            pltpu.VMEM((256, LENGTH), BF16),
            pltpu.VMEM((2, UROWS, D), F32),
            pltpu.VMEM((2, 64, D), F32),
            pltpu.VMEM((3, 64, D), F32),
            pltpu.VMEM((2, KZ, 8, D), F32),
            pltpu.VMEM((2, KZ, 8, D), F32),
            pltpu.VMEM((2, KZ, 8, D), F32),
            pltpu.VMEM((KG, 3, 16, D), F32),
            pltpu.VMEM((2, 16, D), F32),
            pltpu.VMEM((2, 2, KX, 4, 48, 128), F32),
            pltpu.VMEM((2, 2, KX, 4, 48, 128), F32),
            pltpu.VMEM((2, 2, KX, 4, 48, 128), F32),
            pltpu.VMEM((2, 3, 4, 96, 128), F32),
            pltpu.VMEM((2, 2, KY, 48, 128), F32),
            pltpu.VMEM((2, 2, KY, 48, 128), F32),
            pltpu.VMEM((2, 2, KY, 48, 128), F32),
            dma((3, 2, 2, KX)),
            dma((3, 2, 2, KX)),
            dma((3, 2, 2, KY)),
            dma((3, 2, 2, KY)),
            dma((2,)),
            dma((2,)),
            dma((3, 2, KZ)),
            dma((3, 2, KZ)),
            dma((2, 2, KZ)),
            dma((2, 2, KZ)),
            dma((4, KT)),
            dma((4, KT)),
            dma((4, KG)),
            dma((20,)),
            dma((2,)),
            dma((10,)),
            dma((10,)),
        ],
        compiler_params=pltpu.CompilerParams(
            collective_id=0, has_side_effects=True, vmem_limit_bytes=62 << 20
        ),
        cost_estimate=pl.CostEstimate(flops=20 << 30, bytes_accessed=60 << 20, transcendentals=0),
    )(x, g, sw, dw, ew, aw, jnp.asarray(cosine), jnp.asarray(sine), *vectors)


def finish_kernel(
    go_ref, gi_ref, f_ref, small_ref,
    out_ref, grad_ref, gain_ref, shift_ref, attn_ref, ab_ref, dense_ref, db_ref,
    expand_ref, eb_ref, shrink_ref, sb_ref,
):
    out_ref[...] = go_ref[0].astype(BF16)
    grad_ref[...] = gi_ref[0]

    @pl.when(pl.program_id(0) == 0)
    def _():
        gain_ref[...] = small_ref[0:1, :].reshape(128)
        shift_ref[...] = small_ref[1:2, :].reshape(128)
        db_ref[...] = small_ref[2:3, :].reshape(128)
        sb_ref[...] = small_ref[2:3, :].reshape(128)
        eb_ref[...] = small_ref[3:4, 0:64].reshape(64)
        ab_ref[...] = small_ref[4:7, 0:16]
        shrink_ref[...] = f_ref[0:1024]
        dense_ref[...] = f_ref[2048:2304]
        for k in range(8):
            expand_ref[:, k * 128 : (k + 1) * 128] = f_ref[1024 + k * 128 : 1152 + k * 128].T
        for k in range(6):
            attn_ref[k // 2, :, k % 2 * 128 : (k % 2 + 1) * 128] = (
                f_ref[2304 + k * 128 : 2432 + k * 128].T
            )


def finish(both, pieces, small):
    def whole(*shape):
        return pl.BlockSpec(shape, lambda i: (0,) * len(shape))

    def f32(*shape):
        return jax.ShapeDtypeStruct(shape, F32)

    spec = pl.BlockSpec((512, D), lambda i: (i, 0))
    shapes = (
        (128,), (128,), (3, 128, 256), (3, 16), (256, 128), (128,), (128, 1024), (64,), (1024, 128),
        (128,),
    )
    return pl.pallas_call(
        finish_kernel,
        grid=(2,),
        out_shape=(jax.ShapeDtypeStruct((LENGTH, D), BF16), f32(LENGTH, D))
        + tuple(f32(*shape) for shape in shapes),
        in_specs=[
            pl.BlockSpec((1, 512, D), lambda i: (0, i, 0)),
            pl.BlockSpec((1, 512, D), lambda i: (1, i, 0)),
            whole(3072, 128),
            whole(8, 128),
        ],
        out_specs=(spec, spec) + tuple(whole(*shape) for shape in shapes),
        compiler_params=pltpu.CompilerParams(vmem_limit_bytes=56 << 20),
        cost_estimate=pl.CostEstimate(flops=0, bytes_accessed=28 << 20, transcendentals=0),
    )(both, both, pieces, small)


def per_device(
    inputs, norm_gain, norm_bias, attn_weight, attn_bias, dense_weight, dense_bias,
    expand_weight, expand_bias, shrink_weight, shrink_bias, cotangent,
):
    both, pieces, small = run_layer(
        inputs, cotangent, shrink_weight, dense_weight, expand_weight, attn_weight,
        norm_gain, norm_bias, expand_bias, attn_bias, dense_bias, shrink_bias,
    )
    return finish(both, pieces, small)


def solution(mesh):
    placed = (
        P("dp", None),
        P(),
        P(),
        P(None, None, "tensor"),
        P(None, "tensor"),
        P("tensor", None),
        P(),
        P(None, "tensor"),
        P("tensor"),
        P("tensor", None),
        P(),
        P("dp", None),
    )
    return jax.shard_map(
        per_device,
        mesh=mesh,
        in_specs=placed,
        out_specs=(
            P("dp", None),
            P("dp", None),
            P("dp"),
            P("dp"),
            P(None, "dp", "tensor"),
            P(None, ("tensor", "dp")),
            P("tensor", "dp"),
            P("dp"),
            P("dp", "tensor"),
            P(("tensor", "dp")),
            P("tensor", "dp"),
            P("dp"),
        ),
        check_vma=False,
    )
```

```python
import jax
import jax.numpy as jnp
import numpy as np
from jax import lax
from jax.experimental import pallas as pl
from jax.experimental.pallas import tpu as pltpu
from jax.sharding import PartitionSpec as P

HD = 64
ROT = 32
LENGTH = 1024
D = 2048
F32 = jnp.float32
BF16 = jnp.bfloat16
MESH = pl.DeviceIdType.MESH

rotary_base = 10000.0
norm_eps = 1e-05

CH = 256
UNITS = 16
UROWS = 128
BATCHES = 16
BROWS = 192
KX = 5
KY = 5
KZ = 5
KT = 8
KG = 4
TICKS = 24


def gelu_parts(v):
    th = jnp.tanh(0.7978845608 * (v + 0.044715 * v * v * v))
    return th, 0.5 * (1.0 + th)


def layer_kernel(
    x_hbm, g_hbm, sw_hbm, dw_hbm, ew_hbm, aw_hbm, cos_hbm, sin_hbm, gain_hbm, shift_hbm, eb_hbm, ab_hbm, db_hbm, sb_hbm,
    all_ref, f_ref, small_ref,
    vec_ref, gain_ref, shift_ref, eb_ref, ab_ref, db_ref, sb_ref, xo_ref, g_ref, n_ref, act_ref, att_ref, gh_ref, gp_ref, q_ref, k_ref, v_ref, ga_ref,
    st_ref, top_ref, sum_ref, dq_ref, dk_ref, dv_ref, km_ref, qm_ref, gm_ref, pm_ref, dl_ref, ds_ref, cos_ref, sin_ref, sw_ref, dw_ref, ew_ref, aw_ref, gs_ref,
    va, vb, vc, vd, ve,
    stream, turned, part, core_in, mine, zp, zd, zb, zg, done,
    xp, xd, xb, mid, yp, yd, yb,
    xsend, xrecv, ysend, yrecv, csend, crecv, zsend, zrecv, gsend, grecv, ssend, srecv, lsem,
    isem, osem, vsend, vrecv,
):
    dp = lax.axis_index("dp")
    tn = lax.axis_index("tensor")
    x, y, c, z = dp % 4, dp // 4, tn % 2, tn // 2

    def side(axis, sg):
        if axis == 0:
            return (y * 4 + (x + sg + 4) % 4, tn)
        if axis == 1:
            return (((y + sg + 4) % 4) * 4 + x, tn)
        if axis == 2:
            return (dp, ((z + sg + 4) % 4) * 2 + c)
        return (dp, z * 2 + 1 - c)

    def load(k):
        rows = pl.ds((k % 4) * CH, CH)
        src, dst = (
            (x_hbm.at[rows], n_ref.at[rows])
            if k < 4
            else (g_hbm.at[rows], g_ref.at[rows])
            if k < 8
            else (
                (sw_hbm, sw_ref),
                (dw_hbm, dw_ref),
                (ew_hbm, ew_ref),
                (aw_hbm, aw_ref),
                (cos_hbm, cos_ref),
                (sin_hbm, sin_ref),
                (gain_hbm, gain_ref),
                (shift_hbm, shift_ref),
                (db_hbm, db_ref),
                (sb_hbm, sb_ref),
                (eb_hbm, eb_ref),
                (ab_hbm, ab_ref),
            )[k - 8]
        )
        return pltpu.make_async_copy(src, dst, isem.at[k])

    for k in (0, 14, 15, 16, 17, 18, 19, 10, 11):
        load(k).start()

    SIDES = [(0, 1), (0, -1), (0, 2), (1, 1), (1, -1), (1, 2), (2, 1), (2, -1), (2, 2), (3, 0)]
    barrier = pltpu.get_barrier_semaphore()
    for axis, sg in SIDES:
        pl.semaphore_signal(barrier, inc=1, device_id=side(axis, sg), device_id_type=MESH)

    gs_ref[...] = jnp.zeros_like(gs_ref)

    def remote(src, dst, ssem, rsem, to):
        return pltpu.make_async_remote_copy(
            src_ref=src, dst_ref=dst, send_sem=ssem, recv_sem=rsem, device_id=to, device_id_type=MESH
        )

    def within(i, n):
        return (i >= 0) & (i < n)

    def when(cond, body, *args):
        pl.when(cond)(lambda: body(*args))

    NT = (((1,), (1,)), ((), ()))
    SG = (1, -1)
    HALVES = (0, 1)

    def rows_of(b, h, hh):
        return pl.ds(pl.multiple_of((b % 4) * BROWS + h * 96 + hh * 48, 8), 48)

    def own_rows(b, h, piece, hh):
        return (
            stream.at[:, piece, rows_of(b, h, hh)]
            if h == 0
            else stream.at[piece, :, rows_of(b, h, hh)]
        )

    def first(kind, h, d, b):
        a = (x, y)[h]
        sg = SG[d]
        slot = b % KX
        sems = (xsend.at[kind, h, d, slot], xrecv.at[kind, h, d, slot], side(h, sg))
        if kind == 0:
            return remote(own_rows(b, h, (a + 2) % 4, d), xp.at[h, d, slot], *sems)
        if kind == 1:
            return remote(own_rows(b, h, (a + sg + 4) % 4, 1 - d), xd.at[h, d, slot], *sems)
        return remote(xp.at[h, d, slot], xb.at[h, d, slot], *sems)

    def second(kind, h, d, b):
        a = (y, x)[h]
        sg = SG[d]
        slot = b % KY
        sems = (ysend.at[kind, h, d, slot], yrecv.at[kind, h, d, slot], side(1 - h, sg))
        if kind == 0:
            return remote(mid.at[h, b % 3, (a + 2) % 4, pl.ds(d * 48, 48)], yp.at[h, d, slot], *sems)
        if kind == 1:
            return remote(
                mid.at[h, b % 3, (a + sg + 4) % 4, pl.ds((1 - d) * 48, 48)], yd.at[h, d, slot], *sems
            )
        return remote(yp.at[h, d, slot], yb.at[h, d, slot], *sems)

    def each(make, kinds, b):
        for kind in kinds:
            for h in HALVES:
                for d in (0, 1):
                    yield make(kind, h, d, b)

    def x0(b):
        for copy in each(first, (0, 1), b):
            copy.start()

    def x1(b):
        slot = b % KX
        for h in HALVES:
            for d in (0, 1):
                a = (x, y)[h]
                first(0, h, d, b).wait_recv()
                xp[h, d, slot] = xp[h, d, slot] + own_rows(b, h, (a + SG[d] + 4) % 4, d)[...]
                first(2, h, d, b).start()

    def x2(b):
        slot = b % KX
        for h in HALVES:
            a = (x, y)[h]
            for d in (0, 1):
                first(1, h, d, b).wait_recv()
                first(2, h, d, b).wait_recv()
            for hh in (0, 1):
                mid[h, b % 3, :, pl.ds(hh * 48, 48)] = (
                    own_rows(b, h, a, hh)[...] + xb[h, hh, slot] + xd[h, 1 - hh, slot]
                )
            for kind in (0, 1):
                for d in (0, 1):
                    second(kind, h, d, b).start()
        for copy in each(first, (0, 1, 2), b):
            copy.wait_send()

    def x3(b):
        slot = b % KY
        for h in HALVES:
            a = (y, x)[h]
            for d in (0, 1):
                second(0, h, d, b).wait_recv()
                yp[h, d, slot] = (
                    yp[h, d, slot] + mid[h, b % 3, (a + SG[d] + 4) % 4, pl.ds(d * 48, 48)]
                )
                second(2, h, d, b).start()

    def x4(b):
        slot = b % KY
        for h in HALVES:
            a = (y, x)[h]
            for d in (0, 1):
                second(1, h, d, b).wait_recv()
                second(2, h, d, b).wait_recv()
            for hh in (0, 1):
                at = pl.ds(pl.multiple_of(b * BROWS + h * 96 + hh * 48, 8), 48)
                f_ref[at] = mid[h, b % 3, a, pl.ds(hh * 48, 48)] + yb[h, hh, slot] + yd[h, 1 - hh, slot]
        for copy in each(second, (0, 1, 2), b):
            copy.wait_send()

    def zrows(u, piece, hh):
        return mine.at[u % 3, pl.ds(pl.multiple_of(piece * 16 + hh * 8, 8), 8)]

    def along(kind, d, u):
        sg = SG[d]
        slot = u % KZ
        sems = (zsend.at[kind, d, slot], zrecv.at[kind, d, slot], side(2, sg))
        if kind == 0:
            return remote(zrows(u, (z + 2) % 4, d), zp.at[d, slot], *sems)
        if kind == 1:
            return remote(zrows(u, (z + sg + 4) % 4, 1 - d), zd.at[d, slot], *sems)
        return remote(zp.at[d, slot], zb.at[d, slot], *sems)

    def cross(u):
        return remote(
            part.at[u % 2, pl.ds(pl.multiple_of((1 - c) * 64, 64), 64)],
            core_in.at[u % 2],
            csend.at[u % 2],
            crecv.at[u % 2],
            side(3, 0),
        )

    def grow(u, cc, piece, off, size):
        return pl.ds(pl.multiple_of((u % 8) * UROWS + cc * 64 + piece * 16 + off, 8), size)

    def gather1(d, u):
        slot = u % KZ
        return remote(
            done.at[u % 2], zg.at[u % KG, d], gsend.at[0, d, slot], grecv.at[0, d, slot],
            side(2, SG[d]),
        )

    def gather2(d, u):
        slot = u % KZ
        half = pl.ds(d * 8, 8)
        return remote(
            zg.at[u % KG, d, half], zg.at[u % KG, 2, half], gsend.at[1, d, slot],
            grecv.at[1, d, slot], side(2, SG[d]),
        )

    def block_rows(k, u):
        return all_ref.at[u // 8, grow(u, c, (z + (0, -1, 1, 2)[k] + 4) % 4, 0, 16)]

    def block_held(k, u):
        return done.at[u % 2] if k == 0 else zg.at[u % KG, k - 1]

    def twin(k, u):
        slot = u % KT
        return remote(
            block_held(k, u), block_rows(k, u), ssend.at[k, slot], srecv.at[k, slot], side(3, 0)
        )

    def keep(k, u):
        return pltpu.make_async_copy(block_held(k, u), block_rows(k, u), lsem.at[k, u % KG])

    def partial(u, j):
        rows = pl.ds(pl.multiple_of((u % 8) * UROWS, CH), CH)
        cols = pl.ds(pl.multiple_of(j * 1024, 1024), 1024)

        def put(total):
            part[0, :, cols] = total[:UROWS]
            part[1, :, cols] = total[UROWS:]

        @pl.when(u < 8)
        def _():
            put(
                jnp.dot(act_ref[rows, :], sw_ref[:, cols], preferred_element_type=F32)
                + jnp.dot(att_ref[rows, :], dw_ref[:, cols], preferred_element_type=F32)
            )

        @pl.when(u >= 8)
        def _():
            total = lax.dot_general(
                gh_ref[rows, :], ew_ref[cols, :], NT, preferred_element_type=F32
            )
            for k in range(3):
                total += lax.dot_general(
                    gp_ref[k, rows, :], aw_ref[k, cols, :], NT, preferred_element_type=F32
                )
            put(total)

    def z1(u):
        cross(u).wait_recv()

        @pl.loop(0, 2)
        def _(k):
            at = pl.ds(pl.multiple_of(k * 32, 32), 32)
            mine[u % 3, at] = (
                part[u % 2, pl.ds(pl.multiple_of(c * 64 + k * 32, 32), 32)] + core_in[u % 2, at]
            )

        for kind in (0, 1):
            for d in (0, 1):
                along(kind, d, u).start()
        cross(u).wait_send()

    def own_x(u):
        rows = pl.ds(pl.multiple_of((u % 8) * UROWS + c * 64 + z * 16, 16), 16)
        return pltpu.make_async_copy(x_hbm.at[rows], xo_ref.at[u % 2], osem.at[u % 2])

    def z2(u):
        slot = u % KZ
        own_x(u).start()
        for d in (0, 1):
            along(0, d, u).wait_recv()
            zp[d, slot] = zp[d, slot] + zrows(u, (z + SG[d] + 4) % 4, d)[...]
            along(2, d, u).start()

    def z3(u):
        slot = u % KZ
        for d in (0, 1):
            along(1, d, u).wait_recv()
            along(2, d, u).wait_recv()
        whole = jnp.concatenate(
            [zrows(u, z, hh)[...] + zb[hh, slot] + zd[1 - hh, slot] for hh in (0, 1)], axis=0
        )
        rows = pl.ds(pl.multiple_of((u % 8) * UROWS + c * 64 + z * 16, 16), 16)
        own_x(u).wait()
        states = xo_ref[u % 2].astype(F32)

        @pl.when(u < 8)
        def _():
            done[u % 2] = states + whole + vec_ref[2:3, :]

        @pl.when(u >= 8)
        def _():
            center = jnp.mean(states, axis=-1, keepdims=True)
            centred = states - center
            spread = jnp.mean(centred * centred, axis=-1, keepdims=True)
            r = lax.rsqrt(spread + norm_eps)
            zz = centred * r
            e = whole * vec_ref[0:1, :]
            done[u % 2] = g_ref[rows, :].astype(F32) + r * (
                e
                - jnp.mean(e, axis=-1, keepdims=True)
                - zz * jnp.mean(e * zz, axis=-1, keepdims=True)
            )
            gs_ref[0:1, :] += jnp.sum(whole * zz, axis=0, keepdims=True)
            gs_ref[1:2, :] += jnp.sum(whole, axis=0, keepdims=True)

        for d in (0, 1):
            gather1(d, u).start()
        twin(0, u).start()
        keep(0, u).start()
        for kind in (0, 1, 2):
            for d in (0, 1):
                along(kind, d, u).wait_send()

    def z4(u):
        for d in (0, 1):
            gather1(d, u).wait_recv()
        for d in (0, 1):
            gather2(d, u).start()
        for d in (0, 1):
            twin(1 + d, u).start()
            keep(1 + d, u).start()
        keep(0, u).wait()
        for d in (0, 1):
            gather1(d, u).wait_send()
        twin(0, u).wait_send()

    def z5(u):
        for d in (0, 1):
            gather2(d, u).wait_recv()
        twin(3, u).start()
        keep(3, u).start()
        for d in (0, 1):
            gather2(d, u).wait_send()
            twin(1 + d, u).wait_send()
            keep(1 + d, u).wait()

    def z6(u):
        twin(3, u).wait_send()
        keep(3, u).wait()
        for k in range(4):
            twin(k, u).wait_recv()

    def product(left, right, j, q):
        @pl.when(q == 0)
        def _():
            turned[...] = left[...].T

        at = pl.ds(pl.multiple_of((j % 3) * 256, 256), 256)
        both = jnp.dot(
            turned[...],
            right[:, pl.ds(pl.multiple_of(q * 1024, 1024), 1024)],
            preferred_element_type=F32,
        )
        for k in range(8):
            stream[q * 2 + k // 4, k % 4, at] = both[:, k * 128 : (k + 1) * 128]

    def block(j, q):
        cols = pl.ds(pl.multiple_of(j % 4 * 256, 256), 256)
        when(j < 4, product, act_ref.at[:, cols], g_ref, j, q)
        when((j >= 4) & (j < 8), product, gh_ref.at[:, cols], n_ref, j, q)
        when(j == 8, product, att_ref, g_ref, j, q)
        when(j > 8, product, gp_ref.at[jnp.maximum(j - 9, 0)], n_ref, j, q)

    lane = lax.broadcasted_iota(jnp.int32, (1, 256), 1)

    def chunk(i):
        return pl.ds(pl.multiple_of(i * CH, CH), CH)

    def norm_chunk(i):
        @pl.loop(0, 2)
        def _(k):
            rows = pl.ds(pl.multiple_of(i * CH + k * 128, 128), 128)
            states = n_ref[rows, :].astype(F32)
            centred = states - jnp.mean(states, axis=-1, keepdims=True)
            spread = jnp.mean(centred * centred, axis=-1, keepdims=True)
            n_ref[rows, :] = (
                centred * lax.rsqrt(spread + norm_eps) * vec_ref[0:1, :] + vec_ref[1:2, :]
            ).astype(BF16)

    def expand_part(rows, j):
        cols = pl.ds(pl.multiple_of(j * 256, 256), 256)
        hidden = (
            jnp.dot(n_ref[rows, :], ew_ref[:, cols], preferred_element_type=F32)
            + vec_ref[3:4, cols]
        )
        th, half = gelu_parts(hidden)
        act_ref[rows, cols] = (hidden * half).astype(BF16)
        gh_ref[rows, cols] = (
            half
            + (0.5 * 0.7978845608) * hidden * (1.0 - th * th) * (
                1.0 + (3 * 0.044715) * hidden * hidden
            )
        ).astype(BF16)

    def hidden_back(j):
        cols = pl.ds(pl.multiple_of(j * 256, 256), 256)
        back = lax.dot_general(g_ref[...], sw_ref[cols, :], NT, preferred_element_type=F32)
        gh_ref[:, cols] = (back * gh_ref[:, cols].astype(F32)).astype(BF16)

    def turn(values, i, way):
        cosine = cos_ref[chunk(i), :]
        sine = sin_ref[chunk(i), :] * way
        low = lax.broadcasted_iota(jnp.int32, (1, 128), 1) % HD < ROT // 2
        halves = []
        for k in (0, 1):
            v = values[:, k * 128 : (k + 1) * 128]
            swapped = jnp.where(low, -pltpu.roll(v, 128 - ROT // 2, 1), pltpu.roll(v, ROT // 2, 1))
            halves.append(v * cosine + swapped * sine)
        return jnp.concatenate(halves, axis=1)

    def project_chunk(i):
        rows = chunk(i)

        def proj(k):
            return (
                jnp.dot(n_ref[rows, :], aw_ref[k], preferred_element_type=F32)
                + vec_ref[4:5, k * 256 : (k + 1) * 256]
            )

        q_ref[rows, :] = (turn(proj(0), i, 1.0).astype(BF16).astype(F32) * HD**-0.5).astype(BF16)
        k_ref[rows, :] = turn(proj(1), i, 1.0).astype(BF16)
        v_ref[rows, :] = proj(2).astype(BF16)
        ga_ref[rows, :] = lax.dot_general(
            g_ref[rows, :], dw_ref[...], NT, preferred_element_type=F32
        ).astype(BF16)

    HEADS = [slice(h * CH, (h + 1) * CH) for h in range(4)]
    high = lax.broadcasted_iota(jnp.int32, (256, 1), 0)

    def stack_heads(out, values):
        for h in range(4):
            out[HEADS[h], :] = jnp.where(lane // HD == h, values, 0)

    def scores_of(i, j, h, scores):
        allowed = j * CH + lax.broadcasted_iota(
            jnp.int32, (CH, CH), 0
        ) <= i * CH + lax.broadcasted_iota(jnp.int32, (CH, CH), 1)
        return jnp.where(allowed, scores[:, HEADS[h]], -1e30)

    def scores_pair(i, j):
        return lax.dot_general(k_ref[chunk(j), :], qm_ref[...], NT, preferred_element_type=F32)

    def attend_begin(i):
        stack_heads(qm_ref, q_ref[chunk(i), :])
        top_ref[...] = jnp.full_like(top_ref, -1e30)
        sum_ref[...] = jnp.zeros_like(sum_ref)
        dk_ref[...] = jnp.zeros_like(dk_ref)

    def attend_pair(i, j):
        rows = chunk(i)
        scores = scores_pair(i, j)
        values_turned = v_ref[chunk(j), :].T
        for h in range(4):
            part_scores = scores_of(i, j, h, scores)
            old = top_ref[h : h + 1, :]
            top = jnp.maximum(old, jnp.max(part_scores, axis=0, keepdims=True))
            less = jnp.exp(old - top)
            expo = jnp.exp(part_scores - top)
            sum_ref[h : h + 1, :] = sum_ref[h : h + 1, :] * less + jnp.sum(
                expo, axis=0, keepdims=True
            )
            top_ref[h : h + 1, :] = top
            km_ref[:, HEADS[h]] = jnp.where(high // HD == h, values_turned, 0)
            ds_ref[HEADS[h], :] = expo.astype(BF16)
            dk_ref[h * HD : (h + 1) * HD, :] = dk_ref[h * HD : (h + 1) * HD, :] * less
        dk_ref[...] += jnp.dot(km_ref[...], ds_ref[...], preferred_element_type=F32)

        @pl.when(j == i)
        def _():
            for h in range(4):
                at = slice(h * HD, (h + 1) * HD)
                dk_ref[at, :] = dk_ref[at, :] * (1.0 / sum_ref[h : h + 1, :])
            st_ref[0:4, rows] = top_ref[0:4, :] + jnp.log(sum_ref[0:4, :])
            total = dk_ref[...]
            att_ref[rows, :] = total.T.astype(BF16)
            dots = total * ga_ref[rows, :].astype(F32).T
            for h in range(4):
                st_ref[4 + h : 5 + h, rows] = jnp.sum(
                    dots[h * HD : (h + 1) * HD], axis=0, keepdims=True
                )

    def attend_back(j, i):
        rows = chunk(j)
        qrows = chunk(i)
        key = k_ref[rows, :]

        @pl.when(i == j)
        def _():
            keys_turned = key.T
            for h in range(4):
                km_ref[:, HEADS[h]] = jnp.where(high // HD == h, keys_turned, 0)
            dk_ref[...] = jnp.zeros_like(dk_ref)
            dv_ref[...] = jnp.zeros_like(dv_ref)

        stack_heads(qm_ref, q_ref[qrows, :])
        stack_heads(gm_ref, ga_ref[qrows, :])
        scores = lax.dot_general(key, qm_ref[...], NT, preferred_element_type=F32)
        back = lax.dot_general(v_ref[rows, :], gm_ref[...], NT, preferred_element_type=F32)
        for h in range(4):
            chances = jnp.exp(scores_of(i, j, h, scores) - st_ref[h : h + 1, qrows])
            dscore = (chances * (back[:, HEADS[h]] - st_ref[4 + h : 5 + h, qrows])).astype(BF16)
            pm_ref[:, HEADS[h]] = chances.astype(BF16)
            dl_ref[:, HEADS[h]] = dscore
            ds_ref[HEADS[h], :] = dscore
        dk_ref[...] += jnp.dot(dl_ref[...], qm_ref[...], preferred_element_type=F32)
        dv_ref[...] += jnp.dot(pm_ref[...], gm_ref[...], preferred_element_type=F32)
        dq_ref[:, qrows] += jnp.dot(km_ref[...], ds_ref[...], preferred_element_type=F32)

        @pl.when(i == 3)
        def _():
            gp_ref[0, rows, :] = turn(dq_ref[:, rows].T * HD**-0.5, j, -1.0).astype(BF16)
            gp_ref[1, rows, :] = turn(dk_ref[...], j, -1.0).astype(BF16)
            gp_ref[2, rows, :] = dv_ref[...].astype(BF16)

    def token_sums():
        ones = jnp.ones((8, LENGTH), BF16)
        sums = jnp.dot(ones, g_ref[...], preferred_element_type=F32)
        hsum = jnp.dot(ones, gh_ref[...], preferred_element_type=F32)
        psum = [jnp.dot(ones, gp_ref[k], preferred_element_type=F32) for k in range(3)]
        for p in range(16):
            vc[p // 4, p % 4, 2:3] = sums[0:1, p * 128 : (p + 1) * 128]
            vc[p // 4, p % 4, 3:4] = hsum[0:1, p // 2 * 128 : (p // 2 + 1) * 128]
            for k in range(3):
                vc[p // 4, p % 4, 4 + k : 5 + k] = psum[k][0:1, p // 8 * 128 : (p // 8 + 1) * 128]
            vc[p // 4, p % 4, 7:8] = jnp.zeros((1, 128), F32)

    def v_core():
        return remote(va, vb.at[3], vsend.at[0], vrecv.at[0], side(3, 0))

    def v_z(k):
        return remote(va, vb.at[k], vsend.at[1 + k], vrecv.at[1 + k], side(2, (1, -1, 2)[k]))

    def v_x(k):
        sg = (1, -1, 2)[k]
        return remote(vc.at[:, (x + sg + 4) % 4], vd.at[k], vsend.at[4 + k], vrecv.at[4 + k], side(0, sg))

    def v_y(k):
        sg = (1, -1, 2)[k]
        return remote(vd.at[3, (y + sg + 4) % 4], ve.at[k], vsend.at[7 + k], vrecv.at[7 + k], side(1, sg))

    def v0():
        for p in range(16):
            va[p : p + 1] = gs_ref[0:1, p * 128 : (p + 1) * 128]
            va[16 + p : 17 + p] = gs_ref[1:2, p * 128 : (p + 1) * 128]
        v_core().start()

    def v1():
        v_core().wait()
        va[...] = va[...] + vb[3]
        for k in range(3):
            v_z(k).start()

    def v2():
        for k in range(3):
            v_z(k).wait()
        both = va[...] + vb[0] + vb[1] + vb[2]
        for p in range(16):
            vc[p // 4, p % 4, 0:1] = both[p : p + 1]
            vc[p // 4, p % 4, 1:2] = both[16 + p : 17 + p]
        for k in range(3):
            v_x(k).start()

    def v3():
        for k in range(3):
            v_x(k).wait()
        vd[3] = vc[:, x] + vd[0] + vd[1] + vd[2]
        for k in range(3):
            v_y(k).start()

    def v4():
        for k in range(3):
            v_y(k).wait()
        total = vd[3, y] + ve[0] + ve[1] + ve[2]
        small_ref[...] = total
        small_ref[3:4, 0:64] = jnp.where(dp % 2 == 0, total[3:4, 0:64], total[3:4, 64:128])
        mine_of = jnp.zeros((3, 16), F32)
        for k in range(8):
            mine_of = jnp.where(dp % 8 == k, total[4:7, k * 16 : (k + 1) * 16], mine_of)
        small_ref[4:7, 0:16] = mine_of

    def attend_item(k):
        i = at_least(k, 2) + at_least(k, 5) + at_least(k, 9)
        r = k - i * (i + 3) // 2

        @pl.when(r == 0)
        def _():
            project_chunk(i)
            attend_begin(i)

        when(r > 0, attend_pair, i, r - 1)

    def back_item(k):
        j = at_least(k, 4) + at_least(k, 7) + at_least(k, 9)
        attend_back(j, j + k - j * (9 - j) // 2)

    def at_least(k, bound):
        return jnp.where(k >= bound, 1, 0)

    def at_steps(h, steps, body):
        first, count = 0, 0
        for step in steps:
            first += jnp.where(h > step, 1, 0)
            count += jnp.where(h == step, 1, 0)
        pl.loop(first, first + count)(body)

    def stage(t, late, body):
        when((t >= late) & (t < late + 16), body, t - late)

    dq_ref[...] = jnp.zeros_like(dq_ref)
    for k in range(14, 20):
        load(k).wait()
    vec_ref[0:1, :] = gain_ref[...].astype(F32).reshape(1, D)
    vec_ref[1:2, :] = shift_ref[...].astype(F32).reshape(1, D)
    vec_ref[2:3, :] = (db_ref[...].astype(F32) + sb_ref[...].astype(F32)).reshape(1, D)
    vec_ref[3:4, 0:1024] = eb_ref[...].astype(F32).reshape(1, 1024)
    for k in range(3):
        vec_ref[4:5, k * 256 : (k + 1) * 256] = ab_ref[k : k + 1, :].astype(F32)
    pl.semaphore_wait(barrier, len(SIDES))

    @pl.loop(0, TICKS)
    def _(t):
        @pl.loop(0, 4)
        def _(pos):
            h = t * 4 + pos

            @pl.when(pos == 0)
            def _():
                stage(t, 6, z5)
                stage(t, 1, z1)
                stage(t, 8, x4)
                stage(t, 3, x0)
                when(t == 19, v1)
                when(t == 20, v3)

            @pl.when(pos == 1)
            def _():
                stage(t, 7, z6)
                stage(t, 2, z2)
                stage(t, 4, x1)

            @pl.when(pos == 2)
            def _():
                stage(t, 3, z3)
                stage(t, 5, x2)
                when(t == 18, v0)
                when(t == 19, v2)
                when(t == 20, v4)

            @pl.when(pos == 3)
            def _():
                stage(t, 4, z4)
                stage(t, 6, x3)

            @pl.when(t < UNITS + 1)
            def _():
                when((pos > 0) & (pos < 3) & (t % 2 == 0) & (t < UNITS), partial, t, pos - 1)
                when((pos == 2) & (t < UNITS), lambda: cross(t).start())
                w = t - 2
                when(
                    (pos >= 2) & (w >= 0) & (w % 4 < 3),
                    lambda: block(w // 4 * 3 + w % 4, pos - 2),
                )

                @pl.when(h < 4)
                def _():
                    @pl.when(h == 0)
                    def _():
                        load(0).wait()
                        for k in (12, 13, 4, 9, 8):
                            load(k).start()

                    for k in range(1, 4):
                        when(h == k, load(k).wait)
                    norm_chunk(h)

                @pl.when(h == 0)
                def _():
                    load(10).wait()
                    pl.loop(0, 4)(lambda j: expand_part(pl.ds(0, CH), j))
                    for k in (1, 2, 3, 5, 6, 7):
                        load(k).start()
                    for k in (4, 9, 11, 12, 13):
                        load(k).wait()

                @pl.when(h == 3)
                def _():
                    for k in (5, 6, 7):
                        load(k).wait()

                at_steps(h, (3, 4, 6, 7), lambda j: expand_part(pl.ds(CH, LENGTH - CH), j))
                at_steps(h, (0, 0, 5, 5, 8, 9, 11, 12, 13, 14, 15, 16, 17, 18), attend_item)
                at_steps(h, (19, 20, 21, 24), hidden_back)
                at_steps(h, (28, 29, 31, 32, 36, 37, 40, 44, 45, 52), back_item)
                when(h == 53, token_sums)
                when(h == 0, load(8).wait)


def rotary_tables():
    freqs = np.exp(
        -np.arange(ROT // 2).astype(np.float32) * np.float32(2.0 / ROT) * np.log(np.float32(rotary_base))
    ).astype(np.float32)
    angles = np.arange(LENGTH).astype(np.float32)[:, None] * freqs[None, :]
    rest = np.zeros((LENGTH, HD - ROT), np.float32)
    one = np.concatenate([np.cos(angles), np.cos(angles), rest + 1], axis=1)
    two = np.concatenate([np.sin(angles), np.sin(angles), rest], axis=1)
    return (
        np.tile(one, (1, 2)).astype(np.float32),
        np.tile(two, (1, 2)).astype(np.float32),
    )


def run_layer(x, g, sw, dw, ew, aw, *vectors):
    vmem = pl.BlockSpec(memory_space=pltpu.VMEM)
    anym = pl.BlockSpec(memory_space=pl.ANY)
    dma = pltpu.SemaphoreType.DMA
    cosine, sine = rotary_tables()
    return pl.pallas_call(
        layer_kernel,
        out_shape=(
            jax.ShapeDtypeStruct((2, LENGTH, D), F32),
            jax.ShapeDtypeStruct((3072, 128), F32),
            jax.ShapeDtypeStruct((8, 128), F32),
        ),
        in_specs=[anym] * 14,
        out_specs=(anym, vmem, vmem),
        scratch_shapes=[
            pltpu.VMEM((8, D), F32),
            pltpu.VMEM((D,), BF16),
            pltpu.VMEM((D,), BF16),
            pltpu.VMEM((1024,), BF16),
            pltpu.VMEM((3, 256), BF16),
            pltpu.VMEM((D,), BF16),
            pltpu.VMEM((D,), BF16),
            pltpu.VMEM((2, 16, D), BF16),
            pltpu.VMEM((LENGTH, D), BF16),
            pltpu.VMEM((LENGTH, D), BF16),
            pltpu.VMEM((LENGTH, 1024), BF16),
            pltpu.VMEM((LENGTH, 256), BF16),
            pltpu.VMEM((LENGTH, 1024), BF16),
            pltpu.VMEM((3, LENGTH, 256), BF16),
            pltpu.VMEM((LENGTH, 256), BF16),
            pltpu.VMEM((LENGTH, 256), BF16),
            pltpu.VMEM((LENGTH, 256), BF16),
            pltpu.VMEM((LENGTH, 256), BF16),
            pltpu.VMEM((8, LENGTH), F32),
            pltpu.VMEM((8, CH), F32),
            pltpu.VMEM((8, CH), F32),
            pltpu.VMEM((256, LENGTH), F32),
            pltpu.VMEM((CH, 256), F32),
            pltpu.VMEM((CH, 256), F32),
            pltpu.VMEM((256, 4 * CH), BF16),
            pltpu.VMEM((4 * CH, 256), BF16),
            pltpu.VMEM((4 * CH, 256), BF16),
            pltpu.VMEM((CH, 4 * CH), BF16),
            pltpu.VMEM((CH, 4 * CH), BF16),
            pltpu.VMEM((4 * CH, CH), BF16),
            pltpu.VMEM((LENGTH, 128), F32),
            pltpu.VMEM((LENGTH, 128), F32),
            pltpu.VMEM((1024, D), BF16),
            pltpu.VMEM((256, D), BF16),
            pltpu.VMEM((D, 1024), BF16),
            pltpu.VMEM((3, D, 256), BF16),
            pltpu.VMEM((8, D), F32),
            pltpu.VMEM((32, 128), F32),
            pltpu.VMEM((4, 32, 128), F32),
            pltpu.VMEM((4, 4, 8, 128), F32),
            pltpu.VMEM((4, 4, 8, 128), F32),
            pltpu.VMEM((3, 8, 128), F32),
            pltpu.VMEM((4, 4, 4 * BROWS, 128), F32),
            pltpu.VMEM((256, LENGTH), BF16),
            pltpu.VMEM((2, UROWS, D), F32),
            pltpu.VMEM((2, 64, D), F32),
            pltpu.VMEM((3, 64, D), F32),
            pltpu.VMEM((2, KZ, 8, D), F32),
            pltpu.VMEM((2, KZ, 8, D), F32),
            pltpu.VMEM((2, KZ, 8, D), F32),
            pltpu.VMEM((KG, 3, 16, D), F32),
            pltpu.VMEM((2, 16, D), F32),
            pltpu.VMEM((2, 2, KX, 4, 48, 128), F32),
            pltpu.VMEM((2, 2, KX, 4, 48, 128), F32),
            pltpu.VMEM((2, 2, KX, 4, 48, 128), F32),
            pltpu.VMEM((2, 3, 4, 96, 128), F32),
            pltpu.VMEM((2, 2, KY, 48, 128), F32),
            pltpu.VMEM((2, 2, KY, 48, 128), F32),
            pltpu.VMEM((2, 2, KY, 48, 128), F32),
            dma((3, 2, 2, KX)),
            dma((3, 2, 2, KX)),
            dma((3, 2, 2, KY)),
            dma((3, 2, 2, KY)),
            dma((2,)),
            dma((2,)),
            dma((3, 2, KZ)),
            dma((3, 2, KZ)),
            dma((2, 2, KZ)),
            dma((2, 2, KZ)),
            dma((4, KT)),
            dma((4, KT)),
            dma((4, KG)),
            dma((20,)),
            dma((2,)),
            dma((10,)),
            dma((10,)),
        ],
        compiler_params=pltpu.CompilerParams(
            collective_id=0, has_side_effects=True, vmem_limit_bytes=62 << 20
        ),
        cost_estimate=pl.CostEstimate(flops=20 << 30, bytes_accessed=60 << 20, transcendentals=0),
    )(x, g, sw, dw, ew, aw, jnp.asarray(cosine), jnp.asarray(sine), *vectors)


def finish_kernel(
    go_ref, gi_ref, f_ref, small_ref,
    out_ref, grad_ref, gain_ref, shift_ref, attn_ref, ab_ref, dense_ref, db_ref,
    expand_ref, eb_ref, shrink_ref, sb_ref,
):
    out_ref[...] = go_ref[0].astype(BF16)
    grad_ref[...] = gi_ref[0]

    @pl.when(pl.program_id(0) == 0)
    def _():
        gain_ref[...] = small_ref[0:1, :].reshape(128)
        shift_ref[...] = small_ref[1:2, :].reshape(128)
        db_ref[...] = small_ref[2:3, :].reshape(128)
        sb_ref[...] = small_ref[2:3, :].reshape(128)
        eb_ref[...] = small_ref[3:4, 0:64].reshape(64)
        ab_ref[...] = small_ref[4:7, 0:16]
        shrink_ref[...] = f_ref[0:1024]
        dense_ref[...] = f_ref[2048:2304]
        for k in range(8):
            expand_ref[:, k * 128 : (k + 1) * 128] = f_ref[1024 + k * 128 : 1152 + k * 128].T
        for k in range(6):
            attn_ref[k // 2, :, k % 2 * 128 : (k % 2 + 1) * 128] = (
                f_ref[2304 + k * 128 : 2432 + k * 128].T
            )


def finish(both, pieces, small):
    def whole(*shape):
        return pl.BlockSpec(shape, lambda i: (0,) * len(shape))

    def f32(*shape):
        return jax.ShapeDtypeStruct(shape, F32)

    spec = pl.BlockSpec((256, D), lambda i: (i, 0))
    shapes = (
        (128,), (128,), (3, 128, 256), (3, 16), (256, 128), (128,), (128, 1024), (64,), (1024, 128),
        (128,),
    )
    return pl.pallas_call(
        finish_kernel,
        grid=(4,),
        out_shape=(jax.ShapeDtypeStruct((LENGTH, D), BF16), f32(LENGTH, D))
        + tuple(f32(*shape) for shape in shapes),
        in_specs=[
            pl.BlockSpec((1, 256, D), lambda i: (0, i, 0)),
            pl.BlockSpec((1, 256, D), lambda i: (1, i, 0)),
            whole(3072, 128),
            whole(8, 128),
        ],
        out_specs=(spec, spec) + tuple(whole(*shape) for shape in shapes),
        compiler_params=pltpu.CompilerParams(vmem_limit_bytes=56 << 20),
        cost_estimate=pl.CostEstimate(flops=0, bytes_accessed=28 << 20, transcendentals=0),
    )(both, both, pieces, small)


def per_device(
    inputs, norm_gain, norm_bias, attn_weight, attn_bias, dense_weight, dense_bias,
    expand_weight, expand_bias, shrink_weight, shrink_bias, cotangent,
):
    both, pieces, small = run_layer(
        inputs, cotangent, shrink_weight, dense_weight, expand_weight, attn_weight,
        norm_gain, norm_bias, expand_bias, attn_bias, dense_bias, shrink_bias,
    )
    return finish(both, pieces, small)


def solution(mesh):
    placed = (
        P("dp", None),
        P(),
        P(),
        P(None, None, "tensor"),
        P(None, "tensor"),
        P("tensor", None),
        P(),
        P(None, "tensor"),
        P("tensor"),
        P("tensor", None),
        P(),
        P("dp", None),
    )
    return jax.shard_map(
        per_device,
        mesh=mesh,
        in_specs=placed,
        out_specs=(
            P("dp", None),
            P("dp", None),
            P("dp"),
            P("dp"),
            P(None, "dp", "tensor"),
            P(None, ("tensor", "dp")),
            P("tensor", "dp"),
            P("dp"),
            P("dp", "tensor"),
            P(("tensor", "dp")),
            P("tensor", "dp"),
            P("dp"),
        ),
        check_vma=False,
    )
```

```python
import jax
import jax.numpy as jnp
import numpy as np
from jax import lax
from jax.experimental import pallas as pl
from jax.experimental.pallas import tpu as pltpu
from jax.sharding import PartitionSpec as P

HD = 64
ROT = 32
LENGTH = 1024
D = 2048
F32 = jnp.float32
BF16 = jnp.bfloat16
MESH = pl.DeviceIdType.MESH

rotary_base = 10000.0
norm_eps = 1e-05

CH = 256
UNITS = 16
UROWS = 128
BATCHES = 16
BROWS = 192
KX = 5
KY = 5
KZ = 5
KT = 8
KG = 4
TICKS = 24


def gelu_parts(v):
    th = jnp.tanh(0.7978845608 * (v + 0.044715 * v * v * v))
    return th, 0.5 * (1.0 + th)


def layer_kernel(
    x_hbm, g_hbm, sw_hbm, dw_hbm, ew_hbm, aw_hbm, cos_hbm, sin_hbm, gain_hbm, shift_hbm, eb_hbm, ab_hbm, db_hbm, sb_hbm,
    all_ref, f_ref, small_ref,
    vec_ref, gain_ref, shift_ref, eb_ref, ab_ref, db_ref, sb_ref, xo_ref, g_ref, n_ref, act_ref, att_ref, gh_ref, gp_ref, q_ref, k_ref, v_ref, ga_ref,
    st_ref, top_ref, sum_ref, dq_ref, dk_ref, dv_ref, km_ref, qm_ref, gm_ref, pm_ref, dl_ref, ds_ref, cos_ref, sin_ref, sw_ref, dw_ref, ew_ref, aw_ref, gs_ref,
    va, vb, vc, vd, ve,
    stream, turned, part, core_in, mine, zp, zd, zb, zg, done,
    xp, xd, xb, mid, yp, yd, yb,
    xsend, xrecv, ysend, yrecv, csend, crecv, zsend, zrecv, gsend, grecv, ssend, srecv, lsem,
    isem, osem, vsend, vrecv,
):
    dp = lax.axis_index("dp")
    tn = lax.axis_index("tensor")
    x, y, c, z = dp % 4, dp // 4, tn % 2, tn // 2

    def side(axis, sg):
        if axis == 0:
            return (y * 4 + (x + sg + 4) % 4, tn)
        if axis == 1:
            return (((y + sg + 4) % 4) * 4 + x, tn)
        if axis == 2:
            return (dp, ((z + sg + 4) % 4) * 2 + c)
        return (dp, z * 2 + 1 - c)

    def load(k):
        rows = pl.ds((k % 4) * CH, CH)
        src, dst = (
            (x_hbm.at[rows], n_ref.at[rows])
            if k < 4
            else (g_hbm.at[rows], g_ref.at[rows])
            if k < 8
            else (
                (sw_hbm, sw_ref),
                (dw_hbm, dw_ref),
                (ew_hbm, ew_ref),
                (aw_hbm, aw_ref),
                (cos_hbm, cos_ref),
                (sin_hbm, sin_ref),
                (gain_hbm, gain_ref),
                (shift_hbm, shift_ref),
                (db_hbm, db_ref),
                (sb_hbm, sb_ref),
                (eb_hbm, eb_ref),
                (ab_hbm, ab_ref),
            )[k - 8]
        )
        return pltpu.make_async_copy(src, dst, isem.at[k])

    for k in (0, 14, 15, 16, 17, 18, 19, 10, 11):
        load(k).start()

    SIDES = [(0, 1), (0, -1), (0, 2), (1, 1), (1, -1), (1, 2), (2, 1), (2, -1), (2, 2), (3, 0)]
    barrier = pltpu.get_barrier_semaphore()
    for axis, sg in SIDES:
        pl.semaphore_signal(barrier, inc=1, device_id=side(axis, sg), device_id_type=MESH)

    gs_ref[...] = jnp.zeros_like(gs_ref)

    def remote(src, dst, ssem, rsem, to):
        return pltpu.make_async_remote_copy(
            src_ref=src, dst_ref=dst, send_sem=ssem, recv_sem=rsem, device_id=to, device_id_type=MESH
        )

    def within(i, n):
        return (i >= 0) & (i < n)

    def when(cond, body, *args):
        pl.when(cond)(lambda: body(*args))

    NT = (((1,), (1,)), ((), ()))
    SG = (1, -1)
    HALVES = (0, 1)

    def rows_of(b, h, hh):
        return pl.ds(pl.multiple_of((b % 4) * BROWS + h * 96 + hh * 48, 8), 48)

    def own_rows(b, h, piece, hh):
        return (
            stream.at[:, piece, rows_of(b, h, hh)]
            if h == 0
            else stream.at[piece, :, rows_of(b, h, hh)]
        )

    def first(kind, h, d, b):
        a = (x, y)[h]
        sg = SG[d]
        slot = b % KX
        sems = (xsend.at[kind, h, d, slot], xrecv.at[kind, h, d, slot], side(h, sg))
        if kind == 0:
            return remote(own_rows(b, h, (a + 2) % 4, d), xp.at[h, d, slot], *sems)
        if kind == 1:
            return remote(own_rows(b, h, (a + sg + 4) % 4, 1 - d), xd.at[h, d, slot], *sems)
        return remote(xp.at[h, d, slot], xb.at[h, d, slot], *sems)

    def second(kind, h, d, b):
        a = (y, x)[h]
        sg = SG[d]
        slot = b % KY
        sems = (ysend.at[kind, h, d, slot], yrecv.at[kind, h, d, slot], side(1 - h, sg))
        if kind == 0:
            return remote(mid.at[h, b % 3, (a + 2) % 4, pl.ds(d * 48, 48)], yp.at[h, d, slot], *sems)
        if kind == 1:
            return remote(
                mid.at[h, b % 3, (a + sg + 4) % 4, pl.ds((1 - d) * 48, 48)], yd.at[h, d, slot], *sems
            )
        return remote(yp.at[h, d, slot], yb.at[h, d, slot], *sems)

    def each(make, kinds, b):
        for kind in kinds:
            for h in HALVES:
                for d in (0, 1):
                    yield make(kind, h, d, b)

    def x0(b):
        for copy in each(first, (0, 1), b):
            copy.start()

    def x1(b):
        slot = b % KX
        for h in HALVES:
            for d in (0, 1):
                a = (x, y)[h]
                first(0, h, d, b).wait_recv()
                xp[h, d, slot] = xp[h, d, slot] + own_rows(b, h, (a + SG[d] + 4) % 4, d)[...]
                first(2, h, d, b).start()

    def x2(b):
        slot = b % KX
        for h in HALVES:
            a = (x, y)[h]
            for d in (0, 1):
                first(1, h, d, b).wait_recv()
                first(2, h, d, b).wait_recv()
            for hh in (0, 1):
                mid[h, b % 3, :, pl.ds(hh * 48, 48)] = (
                    own_rows(b, h, a, hh)[...] + xb[h, hh, slot] + xd[h, 1 - hh, slot]
                )
            for kind in (0, 1):
                for d in (0, 1):
                    second(kind, h, d, b).start()
        for copy in each(first, (0, 1, 2), b):
            copy.wait_send()

    def x3(b):
        slot = b % KY
        for h in HALVES:
            a = (y, x)[h]
            for d in (0, 1):
                second(0, h, d, b).wait_recv()
                yp[h, d, slot] = (
                    yp[h, d, slot] + mid[h, b % 3, (a + SG[d] + 4) % 4, pl.ds(d * 48, 48)]
                )
                second(2, h, d, b).start()

    def x4(b):
        slot = b % KY
        for h in HALVES:
            a = (y, x)[h]
            for d in (0, 1):
                second(1, h, d, b).wait_recv()
                second(2, h, d, b).wait_recv()
            for hh in (0, 1):
                at = pl.ds(pl.multiple_of(b * BROWS + h * 96 + hh * 48, 8), 48)
                f_ref[at] = mid[h, b % 3, a, pl.ds(hh * 48, 48)] + yb[h, hh, slot] + yd[h, 1 - hh, slot]
        for copy in each(second, (0, 1, 2), b):
            copy.wait_send()

    def zrows(u, piece, hh):
        return mine.at[u % 3, pl.ds(pl.multiple_of(piece * 16 + hh * 8, 8), 8)]

    def along(kind, d, u):
        sg = SG[d]
        slot = u % KZ
        sems = (zsend.at[kind, d, slot], zrecv.at[kind, d, slot], side(2, sg))
        if kind == 0:
            return remote(zrows(u, (z + 2) % 4, d), zp.at[d, slot], *sems)
        if kind == 1:
            return remote(zrows(u, (z + sg + 4) % 4, 1 - d), zd.at[d, slot], *sems)
        return remote(zp.at[d, slot], zb.at[d, slot], *sems)

    def cross(u):
        return remote(
            part.at[u % 2, pl.ds(pl.multiple_of((1 - c) * 64, 64), 64)],
            core_in.at[u % 2],
            csend.at[u % 2],
            crecv.at[u % 2],
            side(3, 0),
        )

    def grow(u, cc, piece, off, size):
        return pl.ds(pl.multiple_of((u % 8) * UROWS + cc * 64 + piece * 16 + off, 8), size)

    def gather1(d, u):
        slot = u % KZ
        return remote(
            done.at[u % 2], zg.at[u % KG, d], gsend.at[0, d, slot], grecv.at[0, d, slot],
            side(2, SG[d]),
        )

    def gather2(d, u):
        slot = u % KZ
        half = pl.ds(d * 8, 8)
        return remote(
            zg.at[u % KG, d, half], zg.at[u % KG, 2, half], gsend.at[1, d, slot],
            grecv.at[1, d, slot], side(2, SG[d]),
        )

    def block_rows(k, u):
        return all_ref.at[u // 8, grow(u, c, (z + (0, -1, 1, 2)[k] + 4) % 4, 0, 16)]

    def block_held(k, u):
        return done.at[u % 2] if k == 0 else zg.at[u % KG, k - 1]

    def twin(k, u):
        slot = u % KT
        return remote(
            block_held(k, u), block_rows(k, u), ssend.at[k, slot], srecv.at[k, slot], side(3, 0)
        )

    def keep(k, u):
        return pltpu.make_async_copy(block_held(k, u), block_rows(k, u), lsem.at[k, u % KG])

    def partial(u, j):
        rows = pl.ds(pl.multiple_of((u % 8) * UROWS, CH), CH)
        cols = pl.ds(pl.multiple_of(j * 1024, 1024), 1024)

        def put(total):
            part[0, :, cols] = total[:UROWS]
            part[1, :, cols] = total[UROWS:]

        @pl.when(u < 8)
        def _():
            put(
                jnp.dot(act_ref[rows, :], sw_ref[:, cols], preferred_element_type=F32)
                + jnp.dot(att_ref[rows, :], dw_ref[:, cols], preferred_element_type=F32)
            )

        @pl.when(u >= 8)
        def _():
            total = lax.dot_general(
                gh_ref[rows, :], ew_ref[cols, :], NT, preferred_element_type=F32
            )
            for k in range(3):
                total += lax.dot_general(
                    gp_ref[k, rows, :], aw_ref[k, cols, :], NT, preferred_element_type=F32
                )
            put(total)

    def z1(u):
        cross(u).wait_recv()

        @pl.loop(0, 2)
        def _(k):
            at = pl.ds(pl.multiple_of(k * 32, 32), 32)
            mine[u % 3, at] = (
                part[u % 2, pl.ds(pl.multiple_of(c * 64 + k * 32, 32), 32)] + core_in[u % 2, at]
            )

        for kind in (0, 1):
            for d in (0, 1):
                along(kind, d, u).start()
        cross(u).wait_send()

    def own_x(u):
        rows = pl.ds(pl.multiple_of((u % 8) * UROWS + c * 64 + z * 16, 16), 16)
        return pltpu.make_async_copy(x_hbm.at[rows], xo_ref.at[u % 2], osem.at[u % 2])

    def z2(u):
        slot = u % KZ
        own_x(u).start()
        for d in (0, 1):
            along(0, d, u).wait_recv()
            zp[d, slot] = zp[d, slot] + zrows(u, (z + SG[d] + 4) % 4, d)[...]
            along(2, d, u).start()

    def z3(u):
        slot = u % KZ

        def send():
            for d in (0, 1):
                gather1(d, u).start()
            twin(0, u).start()
            keep(0, u).start()

        for d in (0, 1):
            along(1, d, u).wait_recv()
            along(2, d, u).wait_recv()
        whole = jnp.concatenate(
            [zrows(u, z, hh)[...] + zb[hh, slot] + zd[1 - hh, slot] for hh in (0, 1)], axis=0
        )
        rows = pl.ds(pl.multiple_of((u % 8) * UROWS + c * 64 + z * 16, 16), 16)
        own_x(u).wait()
        states = xo_ref[u % 2].astype(F32)

        @pl.when(u < 8)
        def _():
            done[u % 2] = states + whole + vec_ref[2:3, :]
            send()

        @pl.when(u >= 8)
        def _():
            center = jnp.mean(states, axis=-1, keepdims=True)
            centred = states - center
            spread = jnp.mean(centred * centred, axis=-1, keepdims=True)
            r = lax.rsqrt(spread + norm_eps)
            zz = centred * r
            e = whole * vec_ref[0:1, :]
            done[u % 2] = g_ref[rows, :].astype(F32) + r * (
                e
                - jnp.mean(e, axis=-1, keepdims=True)
                - zz * jnp.mean(e * zz, axis=-1, keepdims=True)
            )
            send()
            gs_ref[0:1, :] += jnp.sum(whole * zz, axis=0, keepdims=True)
            gs_ref[1:2, :] += jnp.sum(whole, axis=0, keepdims=True)

        for kind in (0, 1, 2):
            for d in (0, 1):
                along(kind, d, u).wait_send()

    def z4(u):
        for d in (0, 1):
            gather1(d, u).wait_recv()
        for d in (0, 1):
            gather2(d, u).start()
        for d in (0, 1):
            twin(1 + d, u).start()
            keep(1 + d, u).start()
        keep(0, u).wait()
        for d in (0, 1):
            gather1(d, u).wait_send()
        twin(0, u).wait_send()

    def z5(u):
        for d in (0, 1):
            gather2(d, u).wait_recv()
        twin(3, u).start()
        keep(3, u).start()
        for d in (0, 1):
            gather2(d, u).wait_send()
            twin(1 + d, u).wait_send()
            keep(1 + d, u).wait()

    def z6(u):
        twin(3, u).wait_send()
        keep(3, u).wait()
        for k in range(4):
            twin(k, u).wait_recv()

    def product(left, right, j, q):
        @pl.when(q == 0)
        def _():
            turned[...] = left[...].T

        at = pl.ds(pl.multiple_of((j % 3) * 256, 256), 256)
        both = jnp.dot(
            turned[...],
            right[:, pl.ds(pl.multiple_of(q * 1024, 1024), 1024)],
            preferred_element_type=F32,
        )
        for k in range(8):
            stream[q * 2 + k // 4, k % 4, at] = both[:, k * 128 : (k + 1) * 128]

    def block(j, q):
        cols = pl.ds(pl.multiple_of(j % 4 * 256, 256), 256)
        when(j < 4, product, act_ref.at[:, cols], g_ref, j, q)
        when((j >= 4) & (j < 8), product, gh_ref.at[:, cols], n_ref, j, q)
        when(j == 8, product, att_ref, g_ref, j, q)
        when(j > 8, product, gp_ref.at[jnp.maximum(j - 9, 0)], n_ref, j, q)

    lane = lax.broadcasted_iota(jnp.int32, (1, 256), 1)

    def chunk(i):
        return pl.ds(pl.multiple_of(i * CH, CH), CH)

    def norm_chunk(i):
        @pl.loop(0, 2)
        def _(k):
            rows = pl.ds(pl.multiple_of(i * CH + k * 128, 128), 128)
            states = n_ref[rows, :].astype(F32)
            centred = states - jnp.mean(states, axis=-1, keepdims=True)
            spread = jnp.mean(centred * centred, axis=-1, keepdims=True)
            n_ref[rows, :] = (
                centred * lax.rsqrt(spread + norm_eps) * vec_ref[0:1, :] + vec_ref[1:2, :]
            ).astype(BF16)

    def expand_part(rows, j):
        cols = pl.ds(pl.multiple_of(j * 256, 256), 256)
        hidden = (
            jnp.dot(n_ref[rows, :], ew_ref[:, cols], preferred_element_type=F32)
            + vec_ref[3:4, cols]
        )
        th, half = gelu_parts(hidden)
        act_ref[rows, cols] = (hidden * half).astype(BF16)
        gh_ref[rows, cols] = (
            half
            + (0.5 * 0.7978845608) * hidden * (1.0 - th * th) * (
                1.0 + (3 * 0.044715) * hidden * hidden
            )
        ).astype(BF16)

    def hidden_back(j):
        cols = pl.ds(pl.multiple_of(j * 256, 256), 256)
        back = lax.dot_general(g_ref[...], sw_ref[cols, :], NT, preferred_element_type=F32)
        gh_ref[:, cols] = (back * gh_ref[:, cols].astype(F32)).astype(BF16)

    def turn(values, i, way):
        cosine = cos_ref[chunk(i), :]
        sine = sin_ref[chunk(i), :] * way
        low = lax.broadcasted_iota(jnp.int32, (1, 128), 1) % HD < ROT // 2
        halves = []
        for k in (0, 1):
            v = values[:, k * 128 : (k + 1) * 128]
            swapped = jnp.where(low, -pltpu.roll(v, 128 - ROT // 2, 1), pltpu.roll(v, ROT // 2, 1))
            halves.append(v * cosine + swapped * sine)
        return jnp.concatenate(halves, axis=1)

    def project_chunk(i):
        rows = chunk(i)

        def proj(k):
            return (
                jnp.dot(n_ref[rows, :], aw_ref[k], preferred_element_type=F32)
                + vec_ref[4:5, k * 256 : (k + 1) * 256]
            )

        q_ref[rows, :] = (turn(proj(0), i, 1.0).astype(BF16).astype(F32) * HD**-0.5).astype(BF16)
        k_ref[rows, :] = turn(proj(1), i, 1.0).astype(BF16)
        v_ref[rows, :] = proj(2).astype(BF16)
        ga_ref[rows, :] = lax.dot_general(
            g_ref[rows, :], dw_ref[...], NT, preferred_element_type=F32
        ).astype(BF16)

    HEADS = [slice(h * CH, (h + 1) * CH) for h in range(4)]
    high = lax.broadcasted_iota(jnp.int32, (256, 1), 0)

    def stack_heads(out, values):
        for h in range(4):
            out[HEADS[h], :] = jnp.where(lane // HD == h, values, 0)

    def scores_of(i, j, h, scores):
        allowed = j * CH + lax.broadcasted_iota(
            jnp.int32, (CH, CH), 0
        ) <= i * CH + lax.broadcasted_iota(jnp.int32, (CH, CH), 1)
        return jnp.where(allowed, scores[:, HEADS[h]], -1e30)

    def scores_pair(i, j):
        return lax.dot_general(k_ref[chunk(j), :], qm_ref[...], NT, preferred_element_type=F32)

    def attend_begin(i):
        stack_heads(qm_ref, q_ref[chunk(i), :])
        top_ref[...] = jnp.full_like(top_ref, -1e30)
        sum_ref[...] = jnp.zeros_like(sum_ref)
        dk_ref[...] = jnp.zeros_like(dk_ref)

    def attend_pair(i, j):
        rows = chunk(i)
        scores = scores_pair(i, j)
        values_turned = v_ref[chunk(j), :].T
        for h in range(4):
            part_scores = scores_of(i, j, h, scores)
            old = top_ref[h : h + 1, :]
            top = jnp.maximum(old, jnp.max(part_scores, axis=0, keepdims=True))
            less = jnp.exp(old - top)
            expo = jnp.exp(part_scores - top)
            sum_ref[h : h + 1, :] = sum_ref[h : h + 1, :] * less + jnp.sum(
                expo, axis=0, keepdims=True
            )
            top_ref[h : h + 1, :] = top
            km_ref[:, HEADS[h]] = jnp.where(high // HD == h, values_turned, 0)
            ds_ref[HEADS[h], :] = expo.astype(BF16)
            dk_ref[h * HD : (h + 1) * HD, :] = dk_ref[h * HD : (h + 1) * HD, :] * less
        dk_ref[...] += jnp.dot(km_ref[...], ds_ref[...], preferred_element_type=F32)

        @pl.when(j == i)
        def _():
            for h in range(4):
                at = slice(h * HD, (h + 1) * HD)
                dk_ref[at, :] = dk_ref[at, :] * (1.0 / sum_ref[h : h + 1, :])
            st_ref[0:4, rows] = top_ref[0:4, :] + jnp.log(sum_ref[0:4, :])
            total = dk_ref[...]
            att_ref[rows, :] = total.T.astype(BF16)
            dots = total * ga_ref[rows, :].astype(F32).T
            for h in range(4):
                st_ref[4 + h : 5 + h, rows] = jnp.sum(
                    dots[h * HD : (h + 1) * HD], axis=0, keepdims=True
                )

    def attend_back(j, i):
        rows = chunk(j)
        qrows = chunk(i)
        key = k_ref[rows, :]

        @pl.when(i == j)
        def _():
            keys_turned = key.T
            for h in range(4):
                km_ref[:, HEADS[h]] = jnp.where(high // HD == h, keys_turned, 0)
            dk_ref[...] = jnp.zeros_like(dk_ref)
            dv_ref[...] = jnp.zeros_like(dv_ref)

        stack_heads(qm_ref, q_ref[qrows, :])
        stack_heads(gm_ref, ga_ref[qrows, :])
        scores = lax.dot_general(key, qm_ref[...], NT, preferred_element_type=F32)
        back = lax.dot_general(v_ref[rows, :], gm_ref[...], NT, preferred_element_type=F32)
        for h in range(4):
            chances = jnp.exp(scores_of(i, j, h, scores) - st_ref[h : h + 1, qrows])
            dscore = (chances * (back[:, HEADS[h]] - st_ref[4 + h : 5 + h, qrows])).astype(BF16)
            pm_ref[:, HEADS[h]] = chances.astype(BF16)
            dl_ref[:, HEADS[h]] = dscore
            ds_ref[HEADS[h], :] = dscore
        dk_ref[...] += jnp.dot(dl_ref[...], qm_ref[...], preferred_element_type=F32)
        dv_ref[...] += jnp.dot(pm_ref[...], gm_ref[...], preferred_element_type=F32)
        dq_ref[:, qrows] += jnp.dot(km_ref[...], ds_ref[...], preferred_element_type=F32)

        @pl.when(i == 3)
        def _():
            gp_ref[0, rows, :] = turn(dq_ref[:, rows].T * HD**-0.5, j, -1.0).astype(BF16)
            gp_ref[1, rows, :] = turn(dk_ref[...], j, -1.0).astype(BF16)
            gp_ref[2, rows, :] = dv_ref[...].astype(BF16)

    def token_sums():
        ones = jnp.ones((8, LENGTH), BF16)
        sums = jnp.dot(ones, g_ref[...], preferred_element_type=F32)
        hsum = jnp.dot(ones, gh_ref[...], preferred_element_type=F32)
        psum = [jnp.dot(ones, gp_ref[k], preferred_element_type=F32) for k in range(3)]
        for p in range(16):
            vc[p // 4, p % 4, 2:3] = sums[0:1, p * 128 : (p + 1) * 128]
            vc[p // 4, p % 4, 3:4] = hsum[0:1, p // 2 * 128 : (p // 2 + 1) * 128]
            for k in range(3):
                vc[p // 4, p % 4, 4 + k : 5 + k] = psum[k][0:1, p // 8 * 128 : (p // 8 + 1) * 128]
            vc[p // 4, p % 4, 7:8] = jnp.zeros((1, 128), F32)

    def v_core():
        return remote(va, vb.at[3], vsend.at[0], vrecv.at[0], side(3, 0))

    def v_z(k):
        return remote(va, vb.at[k], vsend.at[1 + k], vrecv.at[1 + k], side(2, (1, -1, 2)[k]))

    def v_x(k):
        sg = (1, -1, 2)[k]
        return remote(vc.at[:, (x + sg + 4) % 4], vd.at[k], vsend.at[4 + k], vrecv.at[4 + k], side(0, sg))

    def v_y(k):
        sg = (1, -1, 2)[k]
        return remote(vd.at[3, (y + sg + 4) % 4], ve.at[k], vsend.at[7 + k], vrecv.at[7 + k], side(1, sg))

    def v0():
        for p in range(16):
            va[p : p + 1] = gs_ref[0:1, p * 128 : (p + 1) * 128]
            va[16 + p : 17 + p] = gs_ref[1:2, p * 128 : (p + 1) * 128]
        v_core().start()

    def v1():
        v_core().wait()
        va[...] = va[...] + vb[3]
        for k in range(3):
            v_z(k).start()

    def v2():
        for k in range(3):
            v_z(k).wait()
        both = va[...] + vb[0] + vb[1] + vb[2]
        for p in range(16):
            vc[p // 4, p % 4, 0:1] = both[p : p + 1]
            vc[p // 4, p % 4, 1:2] = both[16 + p : 17 + p]
        for k in range(3):
            v_x(k).start()

    def v3():
        for k in range(3):
            v_x(k).wait()
        vd[3] = vc[:, x] + vd[0] + vd[1] + vd[2]
        for k in range(3):
            v_y(k).start()

    def v4():
        for k in range(3):
            v_y(k).wait()
        total = vd[3, y] + ve[0] + ve[1] + ve[2]
        small_ref[...] = total
        small_ref[3:4, 0:64] = jnp.where(dp % 2 == 0, total[3:4, 0:64], total[3:4, 64:128])
        mine_of = jnp.zeros((3, 16), F32)
        for k in range(8):
            mine_of = jnp.where(dp % 8 == k, total[4:7, k * 16 : (k + 1) * 16], mine_of)
        small_ref[4:7, 0:16] = mine_of

    def attend_item(k):
        i = at_least(k, 2) + at_least(k, 5) + at_least(k, 9)
        r = k - i * (i + 3) // 2

        @pl.when(r == 0)
        def _():
            project_chunk(i)
            attend_begin(i)

        when(r > 0, attend_pair, i, r - 1)

    def back_item(k):
        j = at_least(k, 4) + at_least(k, 7) + at_least(k, 9)
        attend_back(j, j + k - j * (9 - j) // 2)

    def at_least(k, bound):
        return jnp.where(k >= bound, 1, 0)

    def at_steps(h, steps, body):
        first, count = 0, 0
        for step in steps:
            first += jnp.where(h > step, 1, 0)
            count += jnp.where(h == step, 1, 0)
        pl.loop(first, first + count)(body)

    def stage(t, late, body):
        when((t >= late) & (t < late + 16), body, t - late)

    dq_ref[...] = jnp.zeros_like(dq_ref)
    for k in range(14, 20):
        load(k).wait()
    vec_ref[0:1, :] = gain_ref[...].astype(F32).reshape(1, D)
    vec_ref[1:2, :] = shift_ref[...].astype(F32).reshape(1, D)
    vec_ref[2:3, :] = (db_ref[...].astype(F32) + sb_ref[...].astype(F32)).reshape(1, D)
    vec_ref[3:4, 0:1024] = eb_ref[...].astype(F32).reshape(1, 1024)
    for k in range(3):
        vec_ref[4:5, k * 256 : (k + 1) * 256] = ab_ref[k : k + 1, :].astype(F32)
    pl.semaphore_wait(barrier, len(SIDES))

    @pl.loop(0, TICKS)
    def _(t):
        @pl.loop(0, 4)
        def _(pos):
            h = t * 4 + pos

            @pl.when(pos == 0)
            def _():
                stage(t, 6, z5)
                stage(t, 1, z1)
                stage(t, 8, x4)
                stage(t, 3, x0)
                when(t == 19, v1)
                when(t == 20, v3)

            @pl.when(pos == 1)
            def _():
                stage(t, 7, z6)
                stage(t, 2, z2)
                stage(t, 4, x1)

            @pl.when(pos == 2)
            def _():
                stage(t, 3, z3)
                stage(t, 5, x2)
                when(t == 18, v0)
                when(t == 19, v2)
                when(t == 20, v4)

            @pl.when(pos == 3)
            def _():
                stage(t, 4, z4)
                stage(t, 6, x3)

            @pl.when(t < UNITS + 1)
            def _():
                when((pos > 0) & (pos < 3) & (t % 2 == 0) & (t < UNITS), partial, t, pos - 1)
                when((pos == 2) & (t < UNITS), lambda: cross(t).start())
                w = t - 2
                when(
                    (pos >= 2) & (w >= 0) & (w % 4 < 3),
                    lambda: block(w // 4 * 3 + w % 4, pos - 2),
                )

                @pl.when(h < 4)
                def _():
                    @pl.when(h == 0)
                    def _():
                        load(0).wait()
                        for k in (12, 13, 4, 9, 8):
                            load(k).start()

                    for k in range(1, 4):
                        when(h == k, load(k).wait)
                    norm_chunk(h)

                @pl.when(h == 0)
                def _():
                    load(10).wait()
                    pl.loop(0, 4)(lambda j: expand_part(pl.ds(0, CH), j))
                    for k in (1, 2, 3, 5, 6, 7):
                        load(k).start()
                    for k in (4, 9, 11, 12, 13):
                        load(k).wait()

                @pl.when(h == 3)
                def _():
                    for k in (5, 6, 7):
                        load(k).wait()

                at_steps(h, (3, 4, 6, 7), lambda j: expand_part(pl.ds(CH, LENGTH - CH), j))
                at_steps(h, (0, 0, 5, 5, 8, 9, 11, 12, 13, 14, 15, 16, 17, 18), attend_item)
                at_steps(h, (19, 20, 21, 24), hidden_back)
                at_steps(h, (28, 29, 31, 32, 36, 37, 40, 44, 45, 52), back_item)
                when(h == 53, token_sums)
                when(h == 0, load(8).wait)


def rotary_tables():
    freqs = np.exp(
        -np.arange(ROT // 2).astype(np.float32) * np.float32(2.0 / ROT) * np.log(np.float32(rotary_base))
    ).astype(np.float32)
    angles = np.arange(LENGTH).astype(np.float32)[:, None] * freqs[None, :]
    rest = np.zeros((LENGTH, HD - ROT), np.float32)
    one = np.concatenate([np.cos(angles), np.cos(angles), rest + 1], axis=1)
    two = np.concatenate([np.sin(angles), np.sin(angles), rest], axis=1)
    return (
        np.tile(one, (1, 2)).astype(np.float32),
        np.tile(two, (1, 2)).astype(np.float32),
    )


def run_layer(x, g, sw, dw, ew, aw, *vectors):
    vmem = pl.BlockSpec(memory_space=pltpu.VMEM)
    anym = pl.BlockSpec(memory_space=pl.ANY)
    dma = pltpu.SemaphoreType.DMA
    cosine, sine = rotary_tables()
    return pl.pallas_call(
        layer_kernel,
        out_shape=(
            jax.ShapeDtypeStruct((2, LENGTH, D), F32),
            jax.ShapeDtypeStruct((3072, 128), F32),
            jax.ShapeDtypeStruct((8, 128), F32),
        ),
        in_specs=[anym] * 14,
        out_specs=(anym, vmem, vmem),
        scratch_shapes=[
            pltpu.VMEM((8, D), F32),
            pltpu.VMEM((D,), BF16),
            pltpu.VMEM((D,), BF16),
            pltpu.VMEM((1024,), BF16),
            pltpu.VMEM((3, 256), BF16),
            pltpu.VMEM((D,), BF16),
            pltpu.VMEM((D,), BF16),
            pltpu.VMEM((2, 16, D), BF16),
            pltpu.VMEM((LENGTH, D), BF16),
            pltpu.VMEM((LENGTH, D), BF16),
            pltpu.VMEM((LENGTH, 1024), BF16),
            pltpu.VMEM((LENGTH, 256), BF16),
            pltpu.VMEM((LENGTH, 1024), BF16),
            pltpu.VMEM((3, LENGTH, 256), BF16),
            pltpu.VMEM((LENGTH, 256), BF16),
            pltpu.VMEM((LENGTH, 256), BF16),
            pltpu.VMEM((LENGTH, 256), BF16),
            pltpu.VMEM((LENGTH, 256), BF16),
            pltpu.VMEM((8, LENGTH), F32),
            pltpu.VMEM((8, CH), F32),
            pltpu.VMEM((8, CH), F32),
            pltpu.VMEM((256, LENGTH), F32),
            pltpu.VMEM((CH, 256), F32),
            pltpu.VMEM((CH, 256), F32),
            pltpu.VMEM((256, 4 * CH), BF16),
            pltpu.VMEM((4 * CH, 256), BF16),
            pltpu.VMEM((4 * CH, 256), BF16),
            pltpu.VMEM((CH, 4 * CH), BF16),
            pltpu.VMEM((CH, 4 * CH), BF16),
            pltpu.VMEM((4 * CH, CH), BF16),
            pltpu.VMEM((LENGTH, 128), F32),
            pltpu.VMEM((LENGTH, 128), F32),
            pltpu.VMEM((1024, D), BF16),
            pltpu.VMEM((256, D), BF16),
            pltpu.VMEM((D, 1024), BF16),
            pltpu.VMEM((3, D, 256), BF16),
            pltpu.VMEM((8, D), F32),
            pltpu.VMEM((32, 128), F32),
            pltpu.VMEM((4, 32, 128), F32),
            pltpu.VMEM((4, 4, 8, 128), F32),
            pltpu.VMEM((4, 4, 8, 128), F32),
            pltpu.VMEM((3, 8, 128), F32),
            pltpu.VMEM((4, 4, 4 * BROWS, 128), F32),
            pltpu.VMEM((256, LENGTH), BF16),
            pltpu.VMEM((2, UROWS, D), F32),
            pltpu.VMEM((2, 64, D), F32),
            pltpu.VMEM((3, 64, D), F32),
            pltpu.VMEM((2, KZ, 8, D), F32),
            pltpu.VMEM((2, KZ, 8, D), F32),
            pltpu.VMEM((2, KZ, 8, D), F32),
            pltpu.VMEM((KG, 3, 16, D), F32),
            pltpu.VMEM((2, 16, D), F32),
            pltpu.VMEM((2, 2, KX, 4, 48, 128), F32),
            pltpu.VMEM((2, 2, KX, 4, 48, 128), F32),
            pltpu.VMEM((2, 2, KX, 4, 48, 128), F32),
            pltpu.VMEM((2, 3, 4, 96, 128), F32),
            pltpu.VMEM((2, 2, KY, 48, 128), F32),
            pltpu.VMEM((2, 2, KY, 48, 128), F32),
            pltpu.VMEM((2, 2, KY, 48, 128), F32),
            dma((3, 2, 2, KX)),
            dma((3, 2, 2, KX)),
            dma((3, 2, 2, KY)),
            dma((3, 2, 2, KY)),
            dma((2,)),
            dma((2,)),
            dma((3, 2, KZ)),
            dma((3, 2, KZ)),
            dma((2, 2, KZ)),
            dma((2, 2, KZ)),
            dma((4, KT)),
            dma((4, KT)),
            dma((4, KG)),
            dma((20,)),
            dma((2,)),
            dma((10,)),
            dma((10,)),
        ],
        compiler_params=pltpu.CompilerParams(
            collective_id=0, has_side_effects=True, vmem_limit_bytes=62 << 20
        ),
        cost_estimate=pl.CostEstimate(flops=20 << 30, bytes_accessed=60 << 20, transcendentals=0),
    )(x, g, sw, dw, ew, aw, jnp.asarray(cosine), jnp.asarray(sine), *vectors)


def finish_kernel(
    go_ref, gi_ref, f_ref, small_ref,
    out_ref, grad_ref, gain_ref, shift_ref, attn_ref, ab_ref, dense_ref, db_ref,
    expand_ref, eb_ref, shrink_ref, sb_ref,
):
    out_ref[...] = go_ref[0].astype(BF16)
    grad_ref[...] = gi_ref[0]

    @pl.when(pl.program_id(0) == 0)
    def _():
        gain_ref[...] = small_ref[0:1, :].reshape(128)
        shift_ref[...] = small_ref[1:2, :].reshape(128)
        db_ref[...] = small_ref[2:3, :].reshape(128)
        sb_ref[...] = small_ref[2:3, :].reshape(128)
        eb_ref[...] = small_ref[3:4, 0:64].reshape(64)
        ab_ref[...] = small_ref[4:7, 0:16]
        shrink_ref[...] = f_ref[0:1024]
        dense_ref[...] = f_ref[2048:2304]
        for k in range(8):
            expand_ref[:, k * 128 : (k + 1) * 128] = f_ref[1024 + k * 128 : 1152 + k * 128].T
        for k in range(6):
            attn_ref[k // 2, :, k % 2 * 128 : (k % 2 + 1) * 128] = (
                f_ref[2304 + k * 128 : 2432 + k * 128].T
            )


def finish(both, pieces, small):
    def whole(*shape):
        return pl.BlockSpec(shape, lambda i: (0,) * len(shape))

    def f32(*shape):
        return jax.ShapeDtypeStruct(shape, F32)

    spec = pl.BlockSpec((256, D), lambda i: (i, 0))
    shapes = (
        (128,), (128,), (3, 128, 256), (3, 16), (256, 128), (128,), (128, 1024), (64,), (1024, 128),
        (128,),
    )
    return pl.pallas_call(
        finish_kernel,
        grid=(4,),
        out_shape=(jax.ShapeDtypeStruct((LENGTH, D), BF16), f32(LENGTH, D))
        + tuple(f32(*shape) for shape in shapes),
        in_specs=[
            pl.BlockSpec((1, 256, D), lambda i: (0, i, 0)),
            pl.BlockSpec((1, 256, D), lambda i: (1, i, 0)),
            whole(3072, 128),
            whole(8, 128),
        ],
        out_specs=(spec, spec) + tuple(whole(*shape) for shape in shapes),
        compiler_params=pltpu.CompilerParams(vmem_limit_bytes=56 << 20),
        cost_estimate=pl.CostEstimate(flops=0, bytes_accessed=28 << 20, transcendentals=0),
    )(both, both, pieces, small)


def per_device(
    inputs, norm_gain, norm_bias, attn_weight, attn_bias, dense_weight, dense_bias,
    expand_weight, expand_bias, shrink_weight, shrink_bias, cotangent,
):
    both, pieces, small = run_layer(
        inputs, cotangent, shrink_weight, dense_weight, expand_weight, attn_weight,
        norm_gain, norm_bias, expand_bias, attn_bias, dense_bias, shrink_bias,
    )
    return finish(both, pieces, small)


def solution(mesh):
    placed = (
        P("dp", None),
        P(),
        P(),
        P(None, None, "tensor"),
        P(None, "tensor"),
        P("tensor", None),
        P(),
        P(None, "tensor"),
        P("tensor"),
        P("tensor", None),
        P(),
        P("dp", None),
    )
    return jax.shard_map(
        per_device,
        mesh=mesh,
        in_specs=placed,
        out_specs=(
            P("dp", None),
            P("dp", None),
            P("dp"),
            P("dp"),
            P(None, "dp", "tensor"),
            P(None, ("tensor", "dp")),
            P("tensor", "dp"),
            P("dp"),
            P("dp", "tensor"),
            P(("tensor", "dp")),
            P("tensor", "dp"),
            P("dp"),
        ),
        check_vma=False,
    )
```
